32 devices in a mesh: rows: 8 (over y, x, core), cols: 4 (over z).
Axes of the slice: x: 2, y: 2, z: 4, core: 2. Of those that a mesh axis runs over, the one named last changes fastest.
Arguments:
- mantissa: bfloat16 [8192, 8192], P('rows', 'cols'), may hold values from 0.5 to 1
- exponents: int32 [512, 64], P('rows'), may hold values from -3 to 1
Outputs:
- spectrum_real: float32 [8192, 8192], P(('rows', 'cols'))
- spectrum_imag: float32 [8192, 8192], P(('rows', 'cols'))
The draws below stay inside these ranges and needn't reach their ends.
Inputs may be any that keep to these rules, and one draw needn't show every extreme that they name: `exponents`: each entry scales its block of 16 rows and 128 columns of the table by 2 to that power.
All inputs are finite; a program needn't handle non-finite values.
Results may differ from the reference program's by a relative error of at most 0.0013.
Values may be sent and summed in bfloat16 or wider, within the bound.
No kernel may reach another device: no remote copies, remote signals or barrier semaphores. Data moves between devices by JAX's collectives and lax.ppermute only.
A program may use at most 128 MiB of HBM per device.

```python
import math
import jax
import jax.numpy as jnp

NR = 8192
NC = 8192


def set_ends(result, key, low, largest):
    spot = [jax.random.randint(jax.random.fold_in(key, axis), (), 0, length) for axis, length in enumerate(result.shape)]
    main_axis = result.shape.index(max(result.shape))
    next_to = spot[:main_axis] + [(spot[main_axis] + 1) % result.shape[main_axis]] + spot[main_axis + 1:]
    return result.at[tuple(spot)].set(low).at[tuple(next_to)].set(largest)


def level_of(rng, shape, split, least, high):
    gain, own = 1.0, jax.random.fold_in(rng, 6)
    for axis_at, parts in split:
        heights = jnp.exp(jax.random.uniform(jax.random.fold_in(own, axis_at), (parts,), jnp.float32, least / len(split), high / len(split)))
        gain = gain * jnp.repeat(heights, shape[axis_at] // parts).reshape([-1 if axis == axis_at else 1 for axis in range(len(shape))])
    return gain


def setup_inputs(seed: int = 0) -> dict:
    keys = jax.random.split(jax.random.key(seed), 3)
    mantissa = jnp.clip(0.5 + 0.5 * jax.random.uniform(keys[0], (NR, NC), jnp.float32) ** level_of(keys[0], (NR, NC), ((0, 8), (1, 4)), -0.2, 0.2), 0.5, 1.0).astype(jnp.bfloat16)
    exponents = set_ends(jax.random.randint(keys[1], (NR // 16, NC // 128), -3, 2), jax.random.fold_in(keys[1], 1), -3, 1).astype(jnp.int32)
    return dict(mantissa=mantissa, exponents=exponents)


def reference(mantissa, exponents):
    scaling = jnp.exp2(exponents.astype(jnp.float32))
    cumulative = (mantissa.astype(jnp.float32).reshape(NR // 16, 16, NC // 128, 128) * scaling[:, None, :, None]).reshape(NR, NC)
    padded = jnp.pad(cumulative, ((1, 0), (1, 0)))
    masses = cumulative - padded[:-1, 1:] - (padded[1:, :-1] - padded[:-1, :-1])
    spectrum = jnp.fft.fft2(masses) / math.sqrt(NR * NC)
    return (jnp.real(spectrum).T.astype(jnp.float32), jnp.imag(spectrum).T.astype(jnp.float32))
```

```python
import functools
import math

import jax
import jax.numpy as jnp
import numpy as np
from jax import lax
from jax.experimental import pallas as pl
from jax.experimental.pallas import tpu as pltpu
from jax.sharding import PartitionSpec as P

LANES = 128
BLOCK_ROWS = 16
BLOCK_COLS = 128
f32 = jnp.float32
bf16 = jnp.bfloat16


def split(value):
    high = value.astype(bf16)
    return high, (value - high.astype(f32)).astype(bf16)


def split_np(table):
    high = np.asarray(table, np.float32).astype(jnp.bfloat16)
    return high, (np.asarray(table, np.float32) - high.astype(np.float32)).astype(jnp.bfloat16)


def product(left, right):
    return lax.dot_general(left, right, (((1,), (0,)), ((), ())), preferred_element_type=f32)


def product3(value, high, low):
    value_high, value_low = split(value)
    return product(value_high, high) + product(value_low, high) + product(value_high, low)


def times(value, angle_part, whole):
    real, imag = value
    angle_part %= whole
    if angle_part == 0:
        return real, imag
    if 4 * angle_part == whole:
        return imag, -real
    if 2 * angle_part == whole:
        return -real, -imag
    if 4 * angle_part == 3 * whole:
        return -imag, real
    if 8 * angle_part == whole:
        c = math.sqrt(0.5)
        return (real + imag) * c, (imag - real) * c
    if 8 * angle_part == 3 * whole:
        c = math.sqrt(0.5)
        return (imag - real) * c, (real + imag) * -c
    c, s = math.cos(2 * math.pi * angle_part / whole), math.sin(2 * math.pi * angle_part / whole)
    return real * c + imag * s, imag * c - real * s


def dft(values, keep=None):
    count = len(values)
    keep = count if keep is None else keep
    if count == 1:
        return values[:keep]
    half = count // 2
    even, odd = dft(values[0::2], min(keep, half)), dft(values[1::2], min(keep, half))
    odd = [times(odd[k], k, count) for k in range(len(odd))]
    low = [(e[0] + o[0], e[1] + o[1]) for e, o in zip(even, odd)]
    high = [(e[0] - o[0], e[1] - o[1]) for e, o in zip(even, odd)]
    return (low + high)[:keep]


def row_kernel(
    cols, group, z_ref, scale_ref, halo_ref, high_ref, low_ref, cos_ref, sin_ref, *refs
):
    pieces, (out_ref, last_ref, table, mixed, stage) = refs[:cols], refs[cols:]
    rows, piece_cols = pieces[0].shape
    halos = halo_ref.shape[0]
    segment = rows // halos
    scales = rows // BLOCK_ROWS
    outer = cos_ref.shape[0]
    slabs, kept = out_ref.shape[:2]
    pad = table.shape[0] - outer * LANES
    z = z_ref[0]
    table[0:pad, :] = jnp.zeros((pad, rows), f32)
    starts = lax.broadcasted_iota(jnp.int32, (rows, LANES), 0) % segment == 0

    for step, piece in enumerate(pieces):
        base = lax.bitwise_xor(z, step) * piece_cols

        def dequantize(block, carry, piece=piece, base=base):
            here = pl.multiple_of(block * LANES, LANES)
            there = pl.multiple_of(base + here, LANES)
            value = piece[:, pl.ds(here, LANES)].astype(f32).reshape(scales, BLOCK_ROWS, LANES)
            value = (value * scale_ref[:, pl.ds(there, LANES)][:, None, :]).reshape(rows, LANES)
            halo = jnp.broadcast_to(
                halo_ref[:, pl.ds(there, LANES)][:, None, :], (halos, segment, LANES)
            ).reshape(rows, LANES)
            above = jnp.where(starts, halo, pltpu.roll(value, 1, 0))
            last_ref[:, pl.ds(there, LANES)] = value.reshape(halos, segment, LANES)[:, segment - 1, :]
            table[pl.ds(pl.multiple_of(pad + there, 8), LANES), :] = (value - above).T
            return carry

        lax.fori_loop(0, piece_cols // LANES, dequantize, 0, unroll=2)

    def mix(index, carry):
        now = table[pl.ds(pad + index, LANES, stride=outer), :]
        before = table[pl.ds(pad + index - 1, LANES, stride=outer), :]
        spun = product3((now - before).T, high_ref[...], low_ref[...])
        real, imag = spun[:, :LANES], spun[:, LANES:]
        cos, sin = cos_ref[pl.ds(index, 1), :], sin_ref[pl.ds(index, 1), :]
        mixed[index, 0] = real * cos + imag * sin
        mixed[index, 1] = imag * cos - real * sin
        return carry

    lax.fori_loop(0, outer, mix, 0, unroll=2)

    inner = outer // slabs

    def finish(tile, carry):
        here = pl.ds(pl.multiple_of(tile * 8, 8), 8)
        for low in range(slabs):
            values = [
                (mixed[high * slabs + low, 0, here, :], mixed[high * slabs + low, 1, here, :])
                for high in range(inner)
            ]
            for k, value in enumerate(dft(values, kept)):
                stage[k, low, 0], stage[k, low, 1] = times(value, low * k, outer)
        for k in range(kept):
            for slab, value in enumerate(dft([(stage[k, low, 0], stage[k, low, 1]) for low in range(slabs)])):
                out_ref[slab, k, 0, here, :], out_ref[slab, k, 1, here, :] = value
        return carry

    lax.fori_loop(0, rows // 8, finish, 0)


def transform_rows(z, pieces, scale, halo, tables, slabs, kept, outer):
    rows, piece_cols = pieces[0].shape
    cols = len(pieces)
    total = cols * piece_cols
    vmem = pl.BlockSpec(memory_space=pltpu.VMEM)
    return pl.pallas_call(
        functools.partial(row_kernel, cols, None),
        out_shape=(
            jax.ShapeDtypeStruct((slabs, kept, 2, rows, LANES), f32),
            jax.ShapeDtypeStruct(halo.shape, f32),
        ),
        in_specs=[pl.BlockSpec(memory_space=pltpu.SMEM)] + [vmem] * (6 + cols),
        out_specs=(vmem, vmem),
        scratch_shapes=[
            pltpu.VMEM((8 + total, rows), f32),
            pltpu.VMEM((outer, 2, rows, LANES), f32),
            pltpu.VMEM((kept, slabs, 2, 8, LANES), f32),
        ],
        compiler_params=pltpu.CompilerParams(vmem_limit_bytes=48 * 1024 * 1024),
        cost_estimate=pl.CostEstimate(
            flops=12 * rows * total * LANES, bytes_accessed=rows * total * 8, transcendentals=0
        ),
        name="row_transform",
    )(z, scale, halo, *tables, *pieces)


def column_kernel(first, high_ref, low_ref, cos_ref, sin_ref, in_ref, out_ref, real, imag):
    sources, _, _, rows, width = in_ref.shape
    count = out_ref.shape[0]
    real[...] = in_ref[:, 0, 0].reshape(sources * rows, width)
    imag[...] = in_ref[:, 0, 1].reshape(sources * rows, width)

    def mix(index, carry):
        here = pl.ds(index, LANES, stride=count)
        value = jnp.concatenate((real[here, :].T, imag[here, :].T), axis=1)
        spun = product3(value, high_ref[...], low_ref[...])
        spun_real, spun_imag = spun[:, :LANES], spun[:, LANES:]
        cos, sin = cos_ref[pl.ds(first + index, 1), :], sin_ref[pl.ds(first + index, 1), :]
        out_ref[index, 0] = spun_real * cos + spun_imag * sin
        out_ref[index, 1] = spun_imag * cos - spun_real * sin
        return carry

    lax.fori_loop(0, count, mix, 0, unroll=2)


def mix_columns(gathered, tables, first, count):
    sources, planes, _, rows, width = gathered.shape
    whole = lambda table: pl.BlockSpec(table.shape, lambda plane: (0, 0))
    return pl.pallas_call(
        functools.partial(column_kernel, first),
        out_shape=jax.ShapeDtypeStruct((count, 2, planes * width, LANES), f32),
        grid=(planes,),
        in_specs=[whole(table) for table in tables]
        + [pl.BlockSpec((sources, 1, 2, rows, width), lambda plane: (0, plane, 0, 0, 0))],
        out_specs=pl.BlockSpec((count, 2, width, LANES), lambda plane: (0, 0, plane, 0)),
        scratch_shapes=[pltpu.VMEM((sources * rows, width), f32)] * 2,
        compiler_params=pltpu.CompilerParams(vmem_limit_bytes=48 * 1024 * 1024),
        cost_estimate=pl.CostEstimate(
            flops=24 * gathered.size * LANES, bytes_accessed=gathered.size * 8, transcendentals=0
        ),
        name="column_mix",
    )(*tables, gathered)


def finish_kernel(outer, *refs):
    parts, (real_ref, imag_ref, stage) = refs[:-3], refs[-3:]
    count = parts[0].shape[0]
    radix = 1 << ((outer.bit_length() - 1) // 2)
    rest = outer // radix

    def finish(tile, carry):
        here = pl.ds(pl.multiple_of(tile * 8, 8), 8)

        def load(index):
            part = parts[index // count]
            return part[index % count, 0, here, :], part[index % count, 1, here, :]

        for low in range(rest):
            values = dft([load(high * rest + low) for high in range(radix)])
            for k, value in enumerate(values):
                stage[k, low, 0], stage[k, low, 1] = times(value, low * k, outer)
        for k in range(radix):
            values = dft([(stage[k, low, 0], stage[k, low, 1]) for low in range(rest)])
            for high, value in enumerate(values):
                column = (k + radix * high) * LANES
                real_ref[here, column : column + LANES], imag_ref[here, column : column + LANES] = value
        return carry

    lax.fori_loop(0, real_ref.shape[0] // 8, finish, 0)


def finish_columns(parts, outer):
    slab = parts[0].shape[2]
    tile = min(32, slab)
    radix = 1 << ((outer.bit_length() - 1) // 2)
    shape = jax.ShapeDtypeStruct((slab, outer * LANES), f32)
    return pl.pallas_call(
        functools.partial(finish_kernel, outer),
        out_shape=(shape, shape),
        grid=(slab // tile,),
        in_specs=[
            pl.BlockSpec((part.shape[0], 2, tile, LANES), lambda step: (0, 0, step, 0)) for part in parts
        ],
        out_specs=(pl.BlockSpec((tile, outer * LANES), lambda step: (step, 0)),) * 2,
        scratch_shapes=[pltpu.VMEM((radix, outer // radix, 2, 8, LANES), f32)],
        compiler_params=pltpu.CompilerParams(vmem_limit_bytes=48 * 1024 * 1024),
        name="column_finish",
    )(*parts)


def local(mantissa, exponents):
    slabs, cols = lax.axis_size("rows"), lax.axis_size("cols")
    half = cols // 2
    z = lax.axis_index("cols")
    kind, side = z % half, z // half
    local_rows, local_cols = mantissa.shape
    total = local_cols * cols
    outer = total // LANES
    slab = total // (slabs * cols)
    inner = outer // slabs
    kept = inner // 2
    lines = local_rows // outer
    kind_lines = lines // half
    chunks = kind_lines * outer // LANES
    count = outer // chunks
    chunk_rows = kind_lines * count

    index = np.arange(LANES)
    angle = 2 * np.pi * (index[:, None] * index[None, :] % LANES) / LANES
    row_matrix = np.concatenate((np.cos(angle), -np.sin(angle)), axis=1)
    column_matrix = np.block([[np.cos(angle), -np.sin(angle)], [np.sin(angle), np.cos(angle)]])
    sides = np.arange(2)[:, None, None] * kept * LANES
    twist = np.arange(outer)[None, :, None] * (index[None, None, :] + sides) % total
    twist = 2 * np.pi * twist / total
    own_side = lambda table: lax.dynamic_index_in_dim(jnp.asarray(table, f32), side, 0, False)
    row_tables = (*split_np(row_matrix), own_side(np.cos(twist)), own_side(np.sin(twist)))
    column_tables = (
        *split_np(column_matrix),
        np.asarray(np.cos(twist[0]) / total, np.float32),
        np.asarray(np.sin(twist[0]) / total, np.float32),
    )

    by_kind = mantissa.reshape(half, kind_lines, chunks, count, local_cols)

    def raw_piece(chunk, step):
        target_kind = lax.bitwise_xor(z, step) % half
        piece = lax.dynamic_index_in_dim(by_kind[:, :, chunk], target_kind, 0, False)
        piece = piece.reshape(chunk_rows, local_cols)
        return trade(piece, step)

    def trade(value, step):
        if step == 0:
            return value
        return lax.ppermute(value, "cols", [(at, at ^ step) for at in range(cols)])

    scaling = jnp.exp2(exponents.astype(f32))
    own_scaling = lax.dynamic_slice_in_dim(scaling, z * (local_cols // BLOCK_COLS), local_cols // BLOCK_COLS, 1)
    ends = mantissa.reshape(lines, outer, local_cols)[:, -1].astype(f32)
    end_scaling = own_scaling.reshape(lines, outer // BLOCK_ROWS, -1)[:, -1]
    ends = (ends.reshape(lines, -1, BLOCK_COLS) * end_scaling[:, :, None]).reshape(lines, local_cols)
    ends = ends.astype(bf16)
    above = lax.ppermute(ends[-1:], "rows", [(at, at + 1) for at in range(slabs - 1)])
    above = jnp.concatenate((above, ends[:-1]), axis=0).reshape(half, kind_lines, local_cols)
    raw = [[raw_piece(chunk, step) for step in range(cols)] for chunk in range(chunks)]
    halos = [
        trade(lax.dynamic_index_in_dim(above, lax.bitwise_xor(z, step) % half, 0, False), step)
        for step in range(cols)
    ]
    halo = jnp.zeros((kind_lines, total), f32)
    for step in range(cols):
        at = lax.bitwise_xor(z, step) * local_cols
        halo = lax.dynamic_update_slice_in_dim(halo, halos[step].astype(f32), at, 1)

    own_rows = lax.dynamic_index_in_dim(
        scaling.reshape(half, kind_lines, chunks, count // BLOCK_ROWS, -1), kind, 0, False
    )
    own_rows = jnp.repeat(own_rows, BLOCK_COLS, axis=-1)

    groups = [
        [row * cols + col for row in range(slabs) for col in range(part * half, (part + 1) * half)]
        for part in range(2)
    ]
    z_word = jnp.full((1,), z, jnp.int32)
    parts = []
    for chunk in range(chunks):
        scale = own_rows[:, chunk].reshape(chunk_rows // BLOCK_ROWS, total)
        spectra, halo = transform_rows(z_word, raw[chunk], scale, halo, row_tables, slabs, kept, outer)
        spectra = spectra.astype(jnp.float16)
        width = min(slab, LANES)
        planes = slab // width
        if slab >= LANES:
            spectra = spectra.reshape(slabs * half, planes, 2, chunk_rows, LANES)
        else:
            spectra = spectra.reshape(slabs, kept, 2, chunk_rows, LANES // slab, slab)
            spectra = spectra.transpose(0, 1, 4, 2, 3, 5).reshape(slabs * half, 1, 2, chunk_rows, slab)
        gathered = lax.all_to_all(
            spectra, ("rows", "cols"), split_axis=0, concat_axis=0, tiled=True, axis_index_groups=groups
        )
        parts.append(mix_columns(gathered.astype(f32), column_tables, chunk * count, count))
    return tuple(finish_columns(parts, outer))


def solution(mesh):
    in_specs = (P("rows", "cols"), P("rows", None))
    out_specs = (P(("rows", "cols"), None), P(("rows", "cols"), None))
    return jax.shard_map(local, mesh=mesh, in_specs=in_specs, out_specs=out_specs, check_vma=False)
```

```python
import functools
import math

import jax
import jax.numpy as jnp
import numpy as np
from jax import lax
from jax.experimental import pallas as pl
from jax.experimental.pallas import tpu as pltpu
from jax.sharding import PartitionSpec as P

LANES = 128
BLOCK_ROWS = 16
BLOCK_COLS = 128
UNITS = 2048
f32 = jnp.float32
bf16 = jnp.bfloat16


def split(value):
    high = value.astype(bf16)
    return high, (value - high.astype(f32)).astype(bf16)


def split_np(table):
    high = np.asarray(table, np.float32).astype(jnp.bfloat16)
    return high, (np.asarray(table, np.float32) - high.astype(np.float32)).astype(jnp.bfloat16)


def product(left, right):
    return lax.dot_general(left, right, (((1,), (0,)), ((), ())), preferred_element_type=f32)


def product3(value, high, low):
    value_high, value_low = split(value)
    if value.shape[1] == LANES:
        both = jnp.concatenate((value_high, value_low), axis=1)
        return product(both, jnp.concatenate((high, high), axis=0)) + product(value_high, low)
    return product(value_high, high) + product(value_low, high) + product(value_high, low)


def times(value, angle_part, whole):
    real, imag = value
    angle_part %= whole
    if angle_part == 0:
        return real, imag
    if 4 * angle_part == whole:
        return imag, -real
    if 2 * angle_part == whole:
        return -real, -imag
    if 4 * angle_part == 3 * whole:
        return -imag, real
    if 8 * angle_part == whole:
        c = math.sqrt(0.5)
        return (real + imag) * c, (imag - real) * c
    if 8 * angle_part == 3 * whole:
        c = math.sqrt(0.5)
        return (imag - real) * c, (real + imag) * -c
    c, s = math.cos(2 * math.pi * angle_part / whole), math.sin(2 * math.pi * angle_part / whole)
    return real * c + imag * s, imag * c - real * s


def dft(values, keep=None):
    count = len(values)
    keep = count if keep is None else keep
    if count == 1:
        return values[:keep]
    half = count // 2
    even, odd = dft(values[0::2], min(keep, half)), dft(values[1::2], min(keep, half))
    odd = [times(odd[k], k, count) for k in range(len(odd))]
    low = [(e[0] + o[0], e[1] + o[1]) for e, o in zip(even, odd)]
    high = [(e[0] - o[0], e[1] - o[1]) for e, o in zip(even, odd)]
    return (low + high)[:keep]


def step_kernel(first, z_ref, scale_ref, before_scale_ref, halo_ref, now_ref, before_ref, out_ref):
    lines, _, segment, width = now_ref.shape[1:]
    groups = segment // BLOCK_ROWS
    starts = lax.broadcasted_iota(jnp.int32, (segment, LANES), 0) == 0

    def take(block, carry):
        here = pl.ds(pl.multiple_of(block * LANES, LANES), LANES)
        last = halo_ref[0, :, here]
        for line in range(lines):
            value = now_ref[0, line, 0, :, here].astype(f32).reshape(groups, BLOCK_ROWS, LANES)
            scale = scale_ref[0, line * groups : (line + 1) * groups, here]
            value = (value * scale[:, None, :]).reshape(segment, LANES)
            ends = before_ref[0, line, 0, segment - BLOCK_ROWS : segment, here].astype(f32)
            ends = ends[BLOCK_ROWS - 1 : BLOCK_ROWS] * before_scale_ref[0, (line + 1) * groups - 1 : (line + 1) * groups, here]
            above = last if first else ends
            last = ends
            change = value - jnp.where(starts, above, pltpu.roll(value, 1, 0))
            out_ref[0, line * segment : (line + 1) * segment, here] = change.astype(jnp.int32).astype(jnp.int16)
        return carry

    lax.fori_loop(0, width // LANES, take, 0)


def step_rows(z, by_kind, scales, halo, chunk):
    kinds, lines, chunks, segment, width = by_kind.shape
    before = (chunk - 1) % chunks
    kind = lambda k, z: lax.rem(lax.bitwise_xor(z[0], k), kinds)
    block = (1, lines, 1, segment, width)
    row_block = (1,) + scales.shape[2:]
    return pl.pallas_call(
        functools.partial(step_kernel, chunk == 0),
        out_shape=jax.ShapeDtypeStruct((kinds, lines * segment, width), jnp.int16),
        grid_spec=pltpu.PrefetchScalarGridSpec(
            num_scalar_prefetch=1,
            grid=(kinds,),
            in_specs=[
                pl.BlockSpec(row_block, lambda k, z: (kind(k, z), 0, 0)),
                pl.BlockSpec(row_block, lambda k, z: (kind(k, z), 0, 0)),
                pl.BlockSpec((1, 1, width), lambda k, z: (kind(k, z), 0, 0)),
                pl.BlockSpec(block, lambda k, z: (kind(k, z), 0, chunk, 0, 0)),
                pl.BlockSpec(block, lambda k, z: (kind(k, z), 0, before, 0, 0)),
            ],
            out_specs=pl.BlockSpec((1, lines * segment, width), lambda k, z: (k, 0, 0)),
        ),
        compiler_params=pltpu.CompilerParams(vmem_limit_bytes=32 * 1024 * 1024),
        cost_estimate=pl.CostEstimate(
            flops=0, bytes_accessed=1024, transcendentals=0
        ),
        name="step_rows",
    )(z, scales[chunk], scales[before], halo, by_kind, by_kind)


SMALLEST = -22
STEPS = 32000.0 / (15 - SMALLEST)


def encode(value):
    size = jnp.maximum(jnp.abs(value), 2.0 ** SMALLEST)
    code = (jnp.log2(size) - SMALLEST) * STEPS + 0.5
    return jnp.where(value < 0, -code, code).astype(jnp.int32).astype(jnp.int16)


def decode(code):
    code = code.astype(jnp.int32).astype(f32)
    size = jnp.abs(code)
    value = jnp.where(size > 0, jnp.exp2(size * (1 / STEPS) + SMALLEST), 0.0)
    return jnp.where(code < 0, -value, value)


def row_kernel(cols, z_ref, high_ref, low_ref, cos_ref, sin_ref, *refs):
    pieces, (out_ref, table, mixed, stage) = refs[:cols], refs[cols:]
    rows, piece_cols = pieces[0].shape
    outer = cos_ref.shape[0]
    slabs, kept = out_ref.shape[:2]
    pad = table.shape[0] - outer * LANES
    z = z_ref[0]
    table[0:pad, :] = jnp.zeros((pad, rows), f32)

    for step, piece in enumerate(pieces):
        base = lax.bitwise_xor(z, step) * piece_cols

        def turn(block, carry, piece=piece, base=base):
            here = pl.multiple_of(block * LANES, LANES)
            value = piece[:, pl.ds(here, LANES)].astype(jnp.int32).astype(f32)
            table[pl.ds(pl.multiple_of(pad + base + here, 8), LANES), :] = value.T
            return carry

        lax.fori_loop(0, piece_cols // LANES, turn, 0, unroll=8)

    def mix(index, carry):
        now = table[pl.ds(pad + index, LANES, stride=outer), :]
        before = table[pl.ds(pad + index - 1, LANES, stride=outer), :]
        spun = product3((now - before).T, high_ref[...], low_ref[...])
        real, imag = spun[:, :LANES], spun[:, LANES:]
        cos, sin = cos_ref[pl.ds(index, 1), :], sin_ref[pl.ds(index, 1), :]
        mixed[index, 0] = real * cos + imag * sin
        mixed[index, 1] = imag * cos - real * sin
        return carry

    lax.fori_loop(0, outer, mix, 0, unroll=8)

    inner = outer // slabs

    def finish(tile, carry):
        here = pl.ds(pl.multiple_of(tile * 16, 16), 16)
        for low in range(slabs):
            values = [
                (mixed[high * slabs + low, 0, here, :], mixed[high * slabs + low, 1, here, :])
                for high in range(inner)
            ]
            for k, value in enumerate(dft(values, kept)):
                stage[k, low, 0], stage[k, low, 1] = times(value, low * k, outer)
        for k in range(kept):
            for slab, value in enumerate(dft([(stage[k, low, 0], stage[k, low, 1]) for low in range(slabs)])):
                out_ref[slab, k, 0, here, :], out_ref[slab, k, 1, here, :] = encode(value[0]), encode(value[1])
        return carry

    lax.fori_loop(0, rows // 16, finish, 0)


def transform_rows(z, pieces, tables, slabs, kept, outer):
    rows, piece_cols = pieces[0].shape
    cols = len(pieces)
    total = cols * piece_cols
    vmem = pl.BlockSpec(memory_space=pltpu.VMEM)
    return pl.pallas_call(
        functools.partial(row_kernel, cols),
        out_shape=jax.ShapeDtypeStruct((slabs, kept, 2, rows, LANES), jnp.int16),
        in_specs=[pl.BlockSpec(memory_space=pltpu.SMEM)] + [vmem] * (4 + cols),
        out_specs=vmem,
        scratch_shapes=[
            pltpu.VMEM((8 + total, rows), f32),
            pltpu.VMEM((outer, 2, rows, LANES), f32),
            pltpu.VMEM((kept, slabs, 2, 16, LANES), f32),
        ],
        compiler_params=pltpu.CompilerParams(vmem_limit_bytes=48 * 1024 * 1024),
        cost_estimate=pl.CostEstimate(
            flops=800 * rows * total * LANES, bytes_accessed=rows * total * 8, transcendentals=0
        ),
        name="row_transform",
    )(z, *tables, *pieces)


def column_kernel(first, high_ref, low_ref, cos_ref, sin_ref, in_ref, out_ref, real, imag):
    sources, _, _, rows, width = in_ref.shape
    count = out_ref.shape[0]

    def take(source, carry):
        here = pl.ds(pl.multiple_of(source * rows, rows), rows)
        real[here, :] = decode(in_ref[source, 0, 0])
        imag[here, :] = decode(in_ref[source, 0, 1])
        return carry

    lax.fori_loop(0, sources, take, 0)

    def mix(index, carry):
        here = pl.ds(index, LANES, stride=count)
        value = jnp.concatenate((real[here, :].T, imag[here, :].T), axis=1)
        spun = product3(value, high_ref[...], low_ref[...])
        spun_real, spun_imag = spun[:, :LANES], spun[:, LANES:]
        cos, sin = cos_ref[pl.ds(first + index, 1), :], sin_ref[pl.ds(first + index, 1), :]
        out_ref[index, 0] = spun_real * cos + spun_imag * sin
        out_ref[index, 1] = spun_imag * cos - spun_real * sin
        return carry

    lax.fori_loop(0, count, mix, 0, unroll=8)


def mix_columns(gathered, tables, first, count):
    sources, planes, _, rows, width = gathered.shape
    whole = lambda table: pl.BlockSpec(table.shape, lambda plane: (0, 0))
    return pl.pallas_call(
        functools.partial(column_kernel, first),
        out_shape=jax.ShapeDtypeStruct((count, 2, planes * width, LANES), f32),
        grid=(planes,),
        in_specs=[whole(table) for table in tables]
        + [pl.BlockSpec((sources, 1, 2, rows, width), lambda plane: (0, plane, 0, 0, 0))],
        out_specs=pl.BlockSpec((count, 2, width, LANES), lambda plane: (0, 0, plane, 0)),
        scratch_shapes=[pltpu.VMEM((sources * rows, width), f32)] * 2,
        compiler_params=pltpu.CompilerParams(vmem_limit_bytes=56 * 1024 * 1024),
        cost_estimate=pl.CostEstimate(
            flops=0, bytes_accessed=1024, transcendentals=0
        ),
        name="column_mix",
    )(*tables, gathered)


def finish_kernel(outer, *refs):
    parts, (real_ref, imag_ref, stage) = refs[:-3], refs[-3:]
    count = parts[0].shape[0]
    radix = 1 << ((outer.bit_length() - 1) // 2)
    rest = outer // radix

    def finish(tile, carry):
        here = pl.ds(pl.multiple_of(tile * 8, 8), 8)

        def load(index):
            part = parts[index // count]
            return part[index % count, 0, here, :], part[index % count, 1, here, :]

        for low in range(rest):
            values = dft([load(high * rest + low) for high in range(radix)])
            for k, value in enumerate(values):
                stage[k, low, 0], stage[k, low, 1] = times(value, low * k, outer)
        for k in range(radix):
            values = dft([(stage[k, low, 0], stage[k, low, 1]) for low in range(rest)])
            for high, value in enumerate(values):
                column = (k + radix * high) * LANES
                real_ref[here, column : column + LANES], imag_ref[here, column : column + LANES] = value
        return carry

    lax.fori_loop(0, real_ref.shape[0] // 8, finish, 0)


def finish_columns(parts, outer):
    slab = parts[0].shape[2]
    tile = min(32, slab)
    radix = 1 << ((outer.bit_length() - 1) // 2)
    shape = jax.ShapeDtypeStruct((slab, outer * LANES), f32)
    return pl.pallas_call(
        functools.partial(finish_kernel, outer),
        out_shape=(shape, shape),
        grid=(slab // tile,),
        in_specs=[
            pl.BlockSpec((part.shape[0], 2, tile, LANES), lambda step: (0, 0, step, 0)) for part in parts
        ],
        out_specs=(pl.BlockSpec((tile, outer * LANES), lambda step: (step, 0)),) * 2,
        scratch_shapes=[pltpu.VMEM((radix, outer // radix, 2, 8, LANES), f32)],
        compiler_params=pltpu.CompilerParams(vmem_limit_bytes=48 * 1024 * 1024),
        name="column_finish",
    )(*parts)


def local(mantissa, exponents):
    slabs, cols = lax.axis_size("rows"), lax.axis_size("cols")
    half = cols // 2
    z = lax.axis_index("cols")
    kind, side = z % half, z // half
    local_rows, local_cols = mantissa.shape
    total = local_cols * cols
    outer = total // LANES
    slab = total // (slabs * cols)
    inner = outer // slabs
    kept = inner // 2
    lines = local_rows // outer
    kind_lines = lines // half
    chunks = kind_lines * outer // LANES
    count = outer // chunks
    chunk_rows = kind_lines * count

    index = np.arange(LANES)
    angle = 2 * np.pi * (index[:, None] * index[None, :] % LANES) / LANES
    row_matrix = np.concatenate((np.cos(angle), -np.sin(angle)), axis=1)
    column_matrix = np.block([[np.cos(angle), -np.sin(angle)], [np.sin(angle), np.cos(angle)]])
    sides = np.arange(2)[:, None, None] * kept * LANES
    twist = np.arange(outer)[None, :, None] * (index[None, None, :] + sides) % total
    twist = 2 * np.pi * twist / total
    own_side = lambda table: lax.dynamic_index_in_dim(jnp.asarray(table, f32), side, 0, False)
    row_tables = (*split_np(row_matrix / UNITS), own_side(np.cos(twist)), own_side(np.sin(twist)))
    column_tables = (
        *split_np(column_matrix),
        np.asarray(np.cos(twist[0]) / total, np.float32),
        np.asarray(np.sin(twist[0]) / total, np.float32),
    )

    scaling = jnp.exp2(exponents.astype(f32)) * UNITS
    scaling = lax.dynamic_slice_in_dim(scaling, z * (local_cols // BLOCK_COLS), local_cols // BLOCK_COLS, 1)
    scales = scaling.reshape(half, kind_lines, chunks, count // BLOCK_ROWS, -1).transpose(2, 0, 1, 3, 4)
    scales = jnp.repeat(scales.reshape(chunks, half, kind_lines * (count // BLOCK_ROWS), -1), BLOCK_COLS, axis=-1)

    by_kind = mantissa.reshape(half, kind_lines, chunks, count, local_cols)
    ends = by_kind[:, -1, -1, -1].astype(f32) * scales[-1, :, -1]
    above = lax.ppermute(ends[-1:].astype(bf16), "rows", [(at, at + 1) for at in range(slabs - 1)])
    halo = jnp.concatenate((above.astype(f32), ends[:-1]), axis=0).reshape(half, 1, local_cols)

    word = jnp.full((1,), z, jnp.int32)
    groups = [
        [row * cols + col for row in range(slabs) for col in range(part * half, (part + 1) * half)]
        for part in range(2)
    ]
    width = min(slab, LANES)
    planes = slab // width

    def exchange(spectra):
        if slab >= LANES:
            spectra = spectra.reshape(slabs * half, planes, 2, chunk_rows, LANES)
        else:
            spectra = spectra.reshape(slabs, kept, 2, chunk_rows, LANES // slab, slab)
            spectra = spectra.transpose(0, 1, 4, 2, 3, 5).reshape(slabs * half, 1, 2, chunk_rows, slab)
        return lax.all_to_all(
            spectra, ("rows", "cols"), split_axis=0, concat_axis=0, tiled=True, axis_index_groups=groups
        )

    order = [*range(1, chunks), 0]
    raw, gathered, parts = {}, {}, {}

    def send(place, source):
        steps = step_rows(source, by_kind, scales, halo, order[place])
        raw[place] = [
            lax.ppermute(steps[step % half], "cols", [(at, at ^ step) for at in range(cols)]) if step else steps[0]
            for step in range(cols)
        ]

    def mix(place):
        chunk = order[place]
        parts[chunk] = mix_columns(gathered[place], column_tables, chunk * count, count)

    for place in range(min(2, chunks)):
        send(place, word)
    for place in range(chunks):
        spectra = transform_rows(word, raw[place], row_tables, slabs, kept, outer)
        if place + 2 < chunks:
            source, spectra = lax.optimization_barrier((word, spectra))
            send(place + 2, source)
        if place >= 1:
            spectra, gathered[place - 1] = lax.optimization_barrier((spectra, gathered[place - 1]))
            mix(place - 1)
        gathered[place] = exchange(spectra)
    mix(chunks - 1)
    return tuple(finish_columns([parts[chunk] for chunk in range(chunks)], outer))


def solution(mesh):
    in_specs = (P("rows", "cols"), P("rows", None))
    out_specs = (P(("rows", "cols"), None), P(("rows", "cols"), None))
    return jax.shard_map(local, mesh=mesh, in_specs=in_specs, out_specs=out_specs, check_vma=False)
```

```python
import functools
import math

import jax
import jax.numpy as jnp
import numpy as np
from jax import lax
from jax.experimental import pallas as pl
from jax.experimental.pallas import tpu as pltpu
from jax.sharding import PartitionSpec as P

LANES = 128
BLOCK_ROWS = 16
BLOCK_COLS = 128
UNITS = 2048
f32 = jnp.float32
bf16 = jnp.bfloat16


def split(value):
    high = value.astype(bf16)
    return high, (value - high.astype(f32)).astype(bf16)


def split_np(table):
    high = np.asarray(table, np.float32).astype(jnp.bfloat16)
    return high, (np.asarray(table, np.float32) - high.astype(np.float32)).astype(jnp.bfloat16)


def product(left, right):
    return lax.dot_general(left, right, (((1,), (0,)), ((), ())), preferred_element_type=f32)


def product3(value, high, low):
    value_high, value_low = split(value)
    if value.shape[1] == LANES:
        both = jnp.concatenate((value_high, value_low), axis=1)
        return product(both, jnp.concatenate((high, high), axis=0)) + product(value_high, low)
    return product(value_high, high) + product(value_low, high) + product(value_high, low)


def times(value, angle_part, whole):
    real, imag = value
    angle_part %= whole
    if angle_part == 0:
        return real, imag
    if 4 * angle_part == whole:
        return imag, -real
    if 2 * angle_part == whole:
        return -real, -imag
    if 4 * angle_part == 3 * whole:
        return -imag, real
    if 8 * angle_part == whole:
        c = math.sqrt(0.5)
        return (real + imag) * c, (imag - real) * c
    if 8 * angle_part == 3 * whole:
        c = math.sqrt(0.5)
        return (imag - real) * c, (real + imag) * -c
    c, s = math.cos(2 * math.pi * angle_part / whole), math.sin(2 * math.pi * angle_part / whole)
    return real * c + imag * s, imag * c - real * s


def dft(values, keep=None):
    count = len(values)
    keep = count if keep is None else keep
    if count == 1:
        return values[:keep]
    half = count // 2
    even, odd = dft(values[0::2], min(keep, half)), dft(values[1::2], min(keep, half))
    odd = [times(odd[k], k, count) for k in range(len(odd))]
    low = [(e[0] + o[0], e[1] + o[1]) for e, o in zip(even, odd)]
    high = [(e[0] - o[0], e[1] - o[1]) for e, o in zip(even, odd)]
    return (low + high)[:keep]


def step_kernel(first, offset, z_ref, scale_ref, before_scale_ref, halo_ref, now_ref, before_ref, out_ref):
    lines, _, segment, width = now_ref.shape[1:]
    groups = segment // BLOCK_ROWS
    size = out_ref.shape[1] // lines
    starts = lax.broadcasted_iota(jnp.int32, (segment, LANES), 0) == 0

    def take(block, carry):
        here = pl.ds(pl.multiple_of(block * LANES, LANES), LANES)
        last = halo_ref[0, :, here]
        for line in range(lines):
            value = now_ref[0, line, 0, :, here].astype(f32).reshape(groups, BLOCK_ROWS, LANES)
            scale = scale_ref[0, line * groups : (line + 1) * groups, here]
            value = (value * scale[:, None, :]).reshape(segment, LANES)
            ends = before_ref[0, line, 0, segment - BLOCK_ROWS : segment, here].astype(f32)
            ends = ends[BLOCK_ROWS - 1 : BLOCK_ROWS] * before_scale_ref[0, (line + 1) * groups - 1 : (line + 1) * groups, here]
            above = last if first else ends
            last = ends
            change = value - jnp.where(starts, above, pltpu.roll(value, 1, 0))
            change = change[offset : offset + size].astype(jnp.int32).astype(jnp.int16)
            out_ref[0, line * size : (line + 1) * size, here] = change
        return carry

    lax.fori_loop(0, width // LANES, take, 0)


def step_rows(z, by_kind, scales, halo, chunk, offset, size):
    kinds, lines, chunks, segment, width = by_kind.shape
    before = (chunk - 1) % chunks
    kind = lambda k, z: lax.rem(lax.bitwise_xor(z[0], k), kinds)
    block = (1, lines, 1, segment, width)
    row_block = (1,) + scales.shape[2:]
    return pl.pallas_call(
        functools.partial(step_kernel, chunk == 0, offset),
        out_shape=jax.ShapeDtypeStruct((kinds, lines * size, width), jnp.int16),
        grid_spec=pltpu.PrefetchScalarGridSpec(
            num_scalar_prefetch=1,
            grid=(kinds,),
            in_specs=[
                pl.BlockSpec(row_block, lambda k, z: (kind(k, z), 0, 0)),
                pl.BlockSpec(row_block, lambda k, z: (kind(k, z), 0, 0)),
                pl.BlockSpec((1, 1, width), lambda k, z: (kind(k, z), 0, 0)),
                pl.BlockSpec(block, lambda k, z: (kind(k, z), 0, chunk, 0, 0)),
                pl.BlockSpec(block, lambda k, z: (kind(k, z), 0, before, 0, 0)),
            ],
            out_specs=pl.BlockSpec((1, lines * size, width), lambda k, z: (k, 0, 0)),
        ),
        compiler_params=pltpu.CompilerParams(vmem_limit_bytes=20 * 1024 * 1024),
        cost_estimate=pl.CostEstimate(
            flops=0, bytes_accessed=1024, transcendentals=0
        ),
        name="step_rows",
    )(z, scales[chunk], scales[before], halo, by_kind, by_kind)


SMALLEST = -22
STEPS = 32000.0 / (15 - SMALLEST)


def encode(value):
    size = jnp.maximum(jnp.abs(value), 2.0 ** SMALLEST)
    code = (jnp.log2(size) - SMALLEST) * STEPS + 0.5
    return jnp.where(value < 0, -code, code).astype(jnp.int32).astype(jnp.int16)


def decode(code):
    code = code.astype(jnp.int32).astype(f32)
    size = jnp.abs(code)
    value = jnp.where(size > 0, jnp.exp2(size * (1 / STEPS) + SMALLEST), 0.0)
    return jnp.where(code < 0, -value, value)


def row_kernel(cols, faces, z_ref, high_ref, low_ref, cos_ref, sin_ref, *refs):
    pieces, (out_ref, table, mixed, stage) = refs[:cols], refs[cols:]
    rows, piece_cols = pieces[0].shape
    outer = cos_ref.shape[0]
    slabs, kept = out_ref.shape[:2]
    pad = table.shape[0] - outer * LANES
    z, first = z_ref[0], z_ref[1]
    table[0:pad, :] = jnp.zeros((pad, rows), f32)

    for step, piece in enumerate(pieces):
        base = lax.bitwise_xor(z, step) * piece_cols

        def turn(block, carry, piece=piece, base=base):
            here = pl.multiple_of(block * LANES, LANES)
            value = piece[:, pl.ds(here, LANES)].astype(jnp.int32).astype(f32)
            table[pl.ds(pl.multiple_of(pad + base + here, 8), LANES), :] = value.T
            return carry

        lax.fori_loop(0, piece_cols // LANES, turn, 0, unroll=8)

    def mix(index, carry):
        now = table[pl.ds(pad + index, LANES, stride=outer), :]
        before = table[pl.ds(pad + index - 1, LANES, stride=outer), :]
        spun = product3((now - before).T, high_ref[...], low_ref[...])
        real, imag = spun[:, :LANES], spun[:, LANES:]
        cos, sin = cos_ref[pl.ds(index, 1), :], sin_ref[pl.ds(index, 1), :]
        mixed[index, 0] = real * cos + imag * sin
        mixed[index, 1] = imag * cos - real * sin
        return carry

    lax.fori_loop(0, outer, mix, 0, unroll=8)

    inner = outer // slabs
    planes = kept // faces

    def finish(tile, carry):
        here = pl.ds(pl.multiple_of(tile * 16, 16), 16)
        for low in range(slabs):
            values = [
                (mixed[high * slabs + low, 0, here, :], mixed[high * slabs + low, 1, here, :])
                for high in range(inner)
            ]
            for k, value in enumerate(dft(values, kept)):
                stage[k, low, 0], stage[k, low, 1] = times(value, low * k, outer)
        for k in range(kept):
            place = lax.bitwise_xor(k // planes, first) * planes + k % planes if faces > 1 else k
            for slab, value in enumerate(dft([(stage[k, low, 0], stage[k, low, 1]) for low in range(slabs)])):
                out_ref[slab, place, 0, here, :], out_ref[slab, place, 1, here, :] = encode(value[0]), encode(value[1])
        return carry

    lax.fori_loop(0, rows // 16, finish, 0)


def transform_rows(z, pieces, tables, slabs, kept, faces, outer):
    rows, piece_cols = pieces[0].shape
    cols = len(pieces)
    total = cols * piece_cols
    vmem = pl.BlockSpec(memory_space=pltpu.VMEM)
    return pl.pallas_call(
        functools.partial(row_kernel, cols, faces),
        out_shape=jax.ShapeDtypeStruct((slabs, kept, 2, rows, LANES), jnp.int16),
        in_specs=[pl.BlockSpec(memory_space=pltpu.SMEM)] + [vmem] * (4 + cols),
        out_specs=vmem,
        scratch_shapes=[
            pltpu.VMEM((8 + total, rows), f32),
            pltpu.VMEM((outer, 2, rows, LANES), f32),
            pltpu.VMEM((kept, slabs, 2, 16, LANES), f32),
        ],
        compiler_params=pltpu.CompilerParams(vmem_limit_bytes=24 * 1024 * 1024),
        cost_estimate=pl.CostEstimate(
            flops=300 * rows * total * LANES, bytes_accessed=rows * total * 8, transcendentals=0
        ),
        name="row_transform",
    )(z, *tables, *pieces)


def column_kernel(first, faces, kind_ref, high_ref, low_ref, cos_ref, sin_ref, *refs):
    in_refs, (out_ref, real, imag) = refs[:faces], refs[faces:]
    sources, _, _, rows, width = in_refs[0].shape
    count = out_ref.shape[0]
    for face, in_ref in enumerate(in_refs):
        slot = lax.bitwise_xor(kind_ref[2], face) if faces > 1 else 0

        def take(source, carry, in_ref=in_ref, slot=slot):
            here = pl.ds(pl.multiple_of((source * faces + slot) * rows, rows), rows)
            real[here, :] = decode(in_ref[source, 0, 0])
            imag[here, :] = decode(in_ref[source, 0, 1])
            return carry

        lax.fori_loop(0, sources, take, 0)

    def mix(index, carry):
        here = pl.ds(index, LANES, stride=count)
        value = jnp.concatenate((real[here, :].T, imag[here, :].T), axis=1)
        spun = product3(value, high_ref[...], low_ref[...])
        spun_real, spun_imag = spun[:, :LANES], spun[:, LANES:]
        cos, sin = cos_ref[pl.ds(first + index, 1), :], sin_ref[pl.ds(first + index, 1), :]
        out_ref[index, 0] = spun_real * cos + spun_imag * sin
        out_ref[index, 1] = spun_imag * cos - spun_real * sin
        return carry

    lax.fori_loop(0, count, mix, 0, unroll=8)


def mix_columns(word, gathered, tables, first, count, planes):
    faces = len(gathered)
    sources, _, _, rows, width = gathered[0].shape
    whole = lambda table: pl.BlockSpec(table.shape, lambda plane: (0, 0))
    return pl.pallas_call(
        functools.partial(column_kernel, first, faces),
        out_shape=jax.ShapeDtypeStruct((count, 2, planes * width, LANES), f32),
        grid=(planes,),
        in_specs=[pl.BlockSpec(memory_space=pltpu.SMEM)]
        + [whole(table) for table in tables]
        + [pl.BlockSpec((sources, 1, 2, rows, width), lambda plane: (0, plane, 0, 0, 0))] * faces,
        out_specs=pl.BlockSpec((count, 2, width, LANES), lambda plane: (0, 0, plane, 0)),
        scratch_shapes=[pltpu.VMEM((faces * sources * rows, width), f32)] * 2,
        compiler_params=pltpu.CompilerParams(vmem_limit_bytes=20 * 1024 * 1024),
        cost_estimate=pl.CostEstimate(flops=0, bytes_accessed=1024, transcendentals=0),
        name="column_mix",
    )(word, *tables, *gathered)


def finish_kernel(outer, *refs):
    parts, (real_ref, imag_ref, stage) = refs[:-3], refs[-3:]
    residues = [(part, index) for part in parts for index in range(part.shape[0])]
    radix = 1 << ((outer.bit_length() - 1) // 2)
    rest = outer // radix

    def finish(tile, carry):
        here = pl.ds(pl.multiple_of(tile * 8, 8), 8)

        def load(index):
            part, own = residues[index]
            return part[own, 0, here, :], part[own, 1, here, :]

        for low in range(rest):
            values = dft([load(high * rest + low) for high in range(radix)])
            for k, value in enumerate(values):
                stage[k, low, 0], stage[k, low, 1] = times(value, low * k, outer)
        for k in range(radix):
            values = dft([(stage[k, low, 0], stage[k, low, 1]) for low in range(rest)])
            for high, value in enumerate(values):
                column = (k + radix * high) * LANES
                real_ref[here, column : column + LANES], imag_ref[here, column : column + LANES] = value
        return carry

    lax.fori_loop(0, real_ref.shape[0] // 8, finish, 0)


def finish_columns(parts, outer):
    slab = parts[0].shape[2]
    tile = min(32, slab)
    radix = 1 << ((outer.bit_length() - 1) // 2)
    shape = jax.ShapeDtypeStruct((slab, outer * LANES), f32)
    return pl.pallas_call(
        functools.partial(finish_kernel, outer),
        out_shape=(shape, shape),
        grid=(slab // tile,),
        in_specs=[
            pl.BlockSpec((part.shape[0], 2, tile, LANES), lambda step: (0, 0, step, 0)) for part in parts
        ],
        out_specs=(pl.BlockSpec((tile, outer * LANES), lambda step: (step, 0)),) * 2,
        scratch_shapes=[pltpu.VMEM((radix, outer // radix, 2, 8, LANES), f32)],
        compiler_params=pltpu.CompilerParams(vmem_limit_bytes=24 * 1024 * 1024),
        name="column_finish",
    )(*parts)


def local(mantissa, exponents):
    slabs, cols = lax.axis_size("rows"), lax.axis_size("cols")
    half = cols // 2
    z = lax.axis_index("cols")
    kind, side = z % half, z // half
    local_rows, local_cols = mantissa.shape
    total = local_cols * cols
    outer = total // LANES
    slab = total // (slabs * cols)
    inner = outer // slabs
    kept = inner // 2
    lines = local_rows // outer
    kind_lines = lines // half
    chunks = kind_lines * outer // LANES
    count = outer // chunks

    index = np.arange(LANES)
    angle = 2 * np.pi * (index[:, None] * index[None, :] % LANES) / LANES
    row_matrix = np.concatenate((np.cos(angle), -np.sin(angle)), axis=1)
    column_matrix = np.block([[np.cos(angle), -np.sin(angle)], [np.sin(angle), np.cos(angle)]])
    sides = np.arange(2)[:, None, None] * kept * LANES
    twist = np.arange(outer)[None, :, None] * (index[None, None, :] + sides) % total
    twist = 2 * np.pi * twist / total
    own_side = lambda table: lax.dynamic_index_in_dim(jnp.asarray(table, f32), side, 0, False)
    row_tables = (*split_np(row_matrix / UNITS), own_side(np.cos(twist)), own_side(np.sin(twist)))
    column_tables = (
        *split_np(column_matrix),
        np.asarray(np.cos(twist[0]) / total, np.float32),
        np.asarray(np.sin(twist[0]) / total, np.float32),
    )

    scaling = jnp.exp2(exponents.astype(f32)) * UNITS
    scaling = lax.dynamic_slice_in_dim(scaling, z * (local_cols // BLOCK_COLS), local_cols // BLOCK_COLS, 1)
    scales = scaling.reshape(half, kind_lines, chunks, count // BLOCK_ROWS, -1).transpose(2, 0, 1, 3, 4)
    scales = jnp.repeat(scales.reshape(chunks, half, kind_lines * (count // BLOCK_ROWS), -1), BLOCK_COLS, axis=-1)

    by_kind = mantissa.reshape(half, kind_lines, chunks, count, local_cols)
    word = jnp.stack([z, jnp.zeros_like(z), kind])
    word_face = jnp.stack([z, kind, kind])
    groups = [
        [row * cols + col for row in range(slabs) for col in range(part * half, (part + 1) * half)]
        for part in range(2)
    ]
    width = min(slab, LANES)
    planes = slab // width

    def exchange(spectra):
        rows = spectra.shape[3]
        if slab >= LANES:
            spectra = spectra.reshape(slabs * half, planes, 2, rows, LANES)
        else:
            spectra = spectra.reshape(slabs, kept, 2, rows, LANES // slab, slab)
            spectra = spectra.transpose(0, 1, 4, 2, 3, 5).reshape(slabs * half, 1, 2, rows, slab)
        return lax.all_to_all(
            spectra, ("rows", "cols"), split_axis=0, concat_axis=0, tiled=True, axis_index_groups=groups
        )

    order = [(c, 0, count) for c in (*range(1, chunks), 0)] if chunks > 1 else [(0, 0, count)]
    places = len(order)
    twice = [False] * places
    raw, sent, gathered, parts = {}, {}, {}, {}

    def send(place, source):
        steps = step_rows(source, by_kind, scales, halo, *order[place])
        raw[place] = [
            lax.ppermute(steps[step % half], "cols", [(at, at ^ step) for at in range(cols)]) if step else steps[0]
            for step in range(cols)
        ]

    def mix(place):
        chunk, offset, size = order[place]
        first = chunk * count + offset
        parts[first] = mix_columns(word, gathered[place], column_tables, first, size, planes)

    halo = jnp.zeros((half, 1, local_cols), f32)
    if places > 1:
        send(0, word)
    last, _ = lax.optimization_barrier((by_kind[:, -1, -1, -1], raw[0][0] if raw else word))
    ends = last.astype(f32) * scales[-1, :, -1]
    above = lax.ppermute(ends[-1:].astype(bf16), "rows", [(at, at + 1) for at in range(slabs - 1)])
    halo = jnp.concatenate((above.astype(f32), ends[:-1]), axis=0).reshape(half, 1, local_cols)

    for place in range(places > 1, min(2, places)):
        send(place, word)
    for place in range(places):
        if 0 < place < places - 1:
            source, *_ = lax.optimization_barrier((word, raw[place][3 % cols]))
            send(place + 1, source)
        spectra = transform_rows(
            word_face if twice[place] else word, raw[place], row_tables, slabs, kept, half if twice[place] else 1, outer
        )
        for before in (place - 1, place - 2):
            if before >= 0 and before == place - (2 if twice[before] else 1):
                spectra, gathered[before] = lax.optimization_barrier((spectra, gathered[before]))
                mix(before)
        if twice[place]:
            over_rows = lax.all_to_all(spectra, "rows", split_axis=0, concat_axis=0, tiled=True)
            other = lax.ppermute(over_rows[:, planes:], "cols", [(at, at ^ 1) for at in range(cols)])
            gathered[place] = [over_rows, other]
        else:
            gathered[place] = [exchange(spectra)]
    for place in range(places):
        first = order[place][0] * count + order[place][1]
        if first not in parts:
            mix(place)
    return tuple(finish_columns([parts[first] for first in sorted(parts)], outer))


def solution(mesh):
    in_specs = (P("rows", "cols"), P("rows", None))
    out_specs = (P(("rows", "cols"), None), P(("rows", "cols"), None))
    return jax.shard_map(local, mesh=mesh, in_specs=in_specs, out_specs=out_specs, check_vma=False)
```

```python
import functools
import math

import jax
import jax.numpy as jnp
import numpy as np
from jax import lax
from jax.experimental import pallas as pl
from jax.experimental.pallas import tpu as pltpu
from jax.sharding import PartitionSpec as P

LANES = 128
BLOCK_ROWS = 16
BLOCK_COLS = 128
UNITS = 2048
PAD = 8
f32 = jnp.float32
bf16 = jnp.bfloat16


def split(value):
    high = value.astype(bf16)
    return high, (value - high.astype(f32)).astype(bf16)


def split_np(table):
    high = np.asarray(table, np.float32).astype(jnp.bfloat16)
    return high, (np.asarray(table, np.float32) - high.astype(np.float32)).astype(jnp.bfloat16)


def product(left, right):
    return lax.dot_general(left, right, (((1,), (0,)), ((), ())), preferred_element_type=f32)


def product3(value, high, low):
    value_high, value_low = split(value)
    if value.shape[1] == LANES:
        both = jnp.concatenate((value_high, value_low), axis=1)
        return product(both, jnp.concatenate((high, high), axis=0)) + product(value_high, low)
    return product(value_high, high) + product(value_low, high) + product(value_high, low)


def times(value, angle_part, whole):
    real, imag = value
    angle_part %= whole
    if angle_part == 0:
        return real, imag
    if 4 * angle_part == whole:
        return imag, -real
    if 2 * angle_part == whole:
        return -real, -imag
    if 4 * angle_part == 3 * whole:
        return -imag, real
    if 8 * angle_part == whole:
        c = math.sqrt(0.5)
        return (real + imag) * c, (imag - real) * c
    if 8 * angle_part == 3 * whole:
        c = math.sqrt(0.5)
        return (imag - real) * c, (real + imag) * -c
    c, s = math.cos(2 * math.pi * angle_part / whole), math.sin(2 * math.pi * angle_part / whole)
    return real * c + imag * s, imag * c - real * s


def dft(values, keep=None):
    count = len(values)
    keep = count if keep is None else keep
    if count == 1:
        return values[:keep]
    half = count // 2
    even, odd = dft(values[0::2], min(keep, half)), dft(values[1::2], min(keep, half))
    odd = [times(odd[k], k, count) for k in range(len(odd))]
    low = [(e[0] + o[0], e[1] + o[1]) for e, o in zip(even, odd)]
    high = [(e[0] - o[0], e[1] - o[1]) for e, o in zip(even, odd)]
    return (low + high)[:keep]


def step_kernel(first, offset, z_ref, scale_ref, before_scale_ref, halo_ref, now_ref, before_ref, *out_refs):
    lines, _, segment, width = now_ref.shape[1:]
    groups = segment // BLOCK_ROWS
    size = out_refs[0].shape[0] // lines
    starts = lax.broadcasted_iota(jnp.int32, (segment, LANES), 0) == 0

    def take(block, carry, out_ref):
        here = pl.ds(pl.multiple_of(block * LANES, LANES), LANES)
        last = halo_ref[0, :, here]
        for line in range(lines):
            value = now_ref[0, line, 0, :, here].astype(f32).reshape(groups, BLOCK_ROWS, LANES)
            scale = scale_ref[0, line * groups : (line + 1) * groups, here]
            value = (value * scale[:, None, :]).reshape(segment, LANES)
            ends = before_ref[0, line, 0, segment - BLOCK_ROWS : segment, here].astype(f32)
            ends = ends[BLOCK_ROWS - 1 : BLOCK_ROWS] * before_scale_ref[0, (line + 1) * groups - 1 : (line + 1) * groups, here]
            above = last if first else ends
            last = ends
            change = value - jnp.where(starts, above, pltpu.roll(value, 1, 0))
            change = change[offset : offset + size].astype(jnp.int32).astype(jnp.int16)
            out_ref[line * size : (line + 1) * size, here] = change
        return carry

    for k, out_ref in enumerate(out_refs):

        @pl.when(pl.program_id(0) == k)
        def _(out_ref=out_ref):
            lax.fori_loop(0, width // LANES, functools.partial(take, out_ref=out_ref), 0)


def step_rows(z, by_kind, scales, halo, chunk, offset, size):
    kinds, lines, chunks, segment, width = by_kind.shape
    before = (chunk - 1) % chunks
    kind = lambda k, z: lax.rem(lax.bitwise_xor(z[0], k), kinds)
    block = (1, lines, 1, segment, width)
    row_block = (1,) + scales.shape[2:]
    return pl.pallas_call(
        functools.partial(step_kernel, chunk == 0, offset),
        out_shape=[jax.ShapeDtypeStruct((lines * size, width), jnp.int16)] * kinds,
        grid_spec=pltpu.PrefetchScalarGridSpec(
            num_scalar_prefetch=1,
            grid=(kinds,),
            in_specs=[
                pl.BlockSpec(row_block, lambda k, z: (kind(k, z), 0, 0)),
                pl.BlockSpec(row_block, lambda k, z: (kind(k, z), 0, 0)),
                pl.BlockSpec((1, 1, width), lambda k, z: (kind(k, z), 0, 0)),
                pl.BlockSpec(block, lambda k, z: (kind(k, z), 0, chunk, 0, 0)),
                pl.BlockSpec(block, lambda k, z: (kind(k, z), 0, before, 0, 0)),
            ],
            out_specs=[pl.BlockSpec((lines * size, width), lambda k, z: (0, 0))] * kinds,
        ),
        compiler_params=pltpu.CompilerParams(vmem_limit_bytes=20 * 1024 * 1024),
        cost_estimate=pl.CostEstimate(
            flops=0, bytes_accessed=1024, transcendentals=0
        ),
        name="step_rows",
    )(z, scales[chunk], scales[before], halo, by_kind, by_kind)


SMALLEST = -22
STEPS = 32000.0 / (15 - SMALLEST)


def encode(value):
    size = jnp.maximum(jnp.abs(value), 2.0 ** SMALLEST)
    code = (jnp.log2(size) - SMALLEST) * STEPS + 0.5
    return jnp.where(value < 0, -code, code).astype(jnp.int32).astype(jnp.int16)


def decode(code):
    code = code.astype(jnp.int32).astype(f32)
    size = jnp.abs(code)
    value = jnp.where(size > 0, jnp.exp2(size * (1 / STEPS) + SMALLEST), 0.0)
    return jnp.where(code < 0, -value, value)


def row_kernel(cols, z_ref, high_ref, low_ref, cos_ref, sin_ref, *refs):
    pieces, (out_ref, table, mixed, stage) = refs[:cols], refs[cols:]
    rows, piece_cols = pieces[0].shape
    outer = cos_ref.shape[0]
    slabs, kept = out_ref.shape[:2]
    pad = PAD
    z = z_ref[0]
    table[0:pad, :] = jnp.zeros((pad, rows), f32)

    for step, piece in enumerate(pieces):
        base = lax.bitwise_xor(z, step) * piece_cols

        def turn(block, carry, piece=piece, base=base):
            here = pl.multiple_of(block * LANES, LANES)
            value = piece[:, pl.ds(here, LANES)].astype(jnp.int32).astype(f32)
            table[pl.ds(pl.multiple_of(pad + base + here, 8), LANES), :] = value.T
            return carry

        lax.fori_loop(0, piece_cols // LANES, turn, 0, unroll=8)

    def mix(index, carry):
        now = table[pl.ds(pad + index, LANES, stride=outer), :]
        before = table[pl.ds(pad + index - 1, LANES, stride=outer), :]
        spun = product3((now - before).T, high_ref[...], low_ref[...])
        real, imag = spun[:, :LANES], spun[:, LANES:]
        cos, sin = cos_ref[pl.ds(index, 1), :], sin_ref[pl.ds(index, 1), :]
        mixed[index, 0] = real * cos + imag * sin
        mixed[index, 1] = imag * cos - real * sin
        return carry

    lax.fori_loop(0, outer, mix, 0, unroll=8)

    inner = outer // slabs

    def finish(tile, carry):
        here = pl.ds(pl.multiple_of(tile * 16, 16), 16)
        for low in range(slabs):
            values = [
                (mixed[high * slabs + low, 0, here, :], mixed[high * slabs + low, 1, here, :])
                for high in range(inner)
            ]
            for k, value in enumerate(dft(values, kept)):
                stage[k, low, 0], stage[k, low, 1] = times(value, low * k, outer)
        for k in range(kept):
            for slab, value in enumerate(dft([(stage[k, low, 0], stage[k, low, 1]) for low in range(slabs)])):
                out_ref[slab, k, 0, here, :], out_ref[slab, k, 1, here, :] = encode(value[0]), encode(value[1])
        return carry

    lax.fori_loop(0, rows // 16, finish, 0)


def transform_rows(z, pieces, tables, slabs, kept, outer):
    rows, piece_cols = pieces[0].shape
    cols = len(pieces)
    total = cols * piece_cols
    vmem = pl.BlockSpec(memory_space=pltpu.VMEM)
    return pl.pallas_call(
        functools.partial(row_kernel, cols),
        out_shape=jax.ShapeDtypeStruct((slabs, kept, 2, rows, LANES), jnp.int16),
        in_specs=[pl.BlockSpec(memory_space=pltpu.SMEM)] + [vmem] * (4 + cols),
        out_specs=vmem,
        scratch_shapes=[
            pltpu.VMEM((PAD + total + outer, rows), f32),
            pltpu.VMEM((outer, 2, rows, LANES), f32),
            pltpu.VMEM((kept, slabs, 2, 16, LANES), f32),
        ],
        compiler_params=pltpu.CompilerParams(vmem_limit_bytes=24 * 1024 * 1024),
        cost_estimate=pl.CostEstimate(
            flops=300 * rows * total * LANES, bytes_accessed=rows * total * 8, transcendentals=0
        ),
        name="row_transform",
    )(z, *tables, *pieces)


def mix_chunk(first, high_ref, low_ref, cos_ref, sin_ref, in_ref, out_ref, real, imag):
    sources, _, _, rows, width = in_ref.shape
    count = out_ref.shape[0]

    def take(source, carry):
        here = pl.ds(pl.multiple_of(source * rows, rows), rows)
        real[here, :] = decode(in_ref[source, 0, 0])
        imag[here, :] = decode(in_ref[source, 0, 1])
        return carry

    def mix(index, carry):
        here = pl.ds(index, LANES, stride=count)
        value = jnp.concatenate((real[here, :].T, imag[here, :].T), axis=1)
        spun = product3(value, high_ref[...], low_ref[...])
        spun_real, spun_imag = spun[:, :LANES], spun[:, LANES:]
        cos, sin = cos_ref[pl.ds(first + index, 1), :], sin_ref[pl.ds(first + index, 1), :]
        out_ref[index, 0] = spun_real * cos + spun_imag * sin
        out_ref[index, 1] = spun_imag * cos - spun_real * sin
        return carry

    lax.fori_loop(0, sources, take, 0)
    lax.fori_loop(0, count, mix, 0, unroll=8)


def mix_columns(gathered, tables, first, count):
    sources, planes, _, rows, width = gathered.shape
    whole = lambda table: pl.BlockSpec(table.shape, lambda plane: (0, 0))
    return pl.pallas_call(
        functools.partial(mix_chunk, first),
        out_shape=jax.ShapeDtypeStruct((count, 2, planes * width, LANES), f32),
        grid=(planes,),
        in_specs=[whole(table) for table in tables]
        + [pl.BlockSpec((sources, 1, 2, rows, width), lambda plane: (0, plane, 0, 0, 0))],
        out_specs=pl.BlockSpec((count, 2, width, LANES), lambda plane: (0, 0, plane, 0)),
        scratch_shapes=[pltpu.VMEM((sources * rows + count, width), f32)] * 2,
        compiler_params=pltpu.CompilerParams(vmem_limit_bytes=20 * 1024 * 1024),
        cost_estimate=pl.CostEstimate(flops=0, bytes_accessed=1024, transcendentals=0),
        name="column_mix",
    )(*tables, gathered)


def finish_kernel(outer, first, high_ref, low_ref, cos_ref, sin_ref, in_ref, *refs):
    parts, (real_ref, imag_ref, stage, mixed, real, imag) = refs[:-6], refs[-6:]
    count = mixed.shape[0]
    size = real_ref.shape[0]
    radix = 1 << ((outer.bit_length() - 1) // 2)
    rest = outer // radix

    @pl.when(pl.program_id(1) == 0)
    def _():
        mix_chunk(first, high_ref, low_ref, cos_ref, sin_ref, in_ref, mixed, real, imag)

    places = [(part, index) for part in parts for index in range(part.shape[0])]
    places[first:first] = [(mixed, index) for index in range(count)]

    def finish(tile, carry):
        here = pl.ds(pl.multiple_of(tile * 8, 8), 8)
        there = pl.ds(pl.multiple_of(pl.program_id(1) * size + tile * 8, 8), 8)

        def load(index):
            part, own = places[index]
            lines = there if part is mixed else here
            return part[own, 0, lines, :], part[own, 1, lines, :]

        for low in range(rest):
            values = dft([load(high * rest + low) for high in range(radix)])
            for k, value in enumerate(values):
                stage[k, low, 0], stage[k, low, 1] = times(value, low * k, outer)
        for k in range(radix):
            values = dft([(stage[k, low, 0], stage[k, low, 1]) for low in range(rest)])
            for high, value in enumerate(values):
                column = (k + radix * high) * LANES
                real_ref[here, column : column + LANES], imag_ref[here, column : column + LANES] = value
        return carry

    lax.fori_loop(0, size // 8, finish, 0)


def finish_columns(gathered, tables, first, count, parts, outer):
    sources, planes, _, rows, width = gathered.shape
    tile = min(32, width)
    steps = width // tile
    radix = 1 << ((outer.bit_length() - 1) // 2)
    shape = jax.ShapeDtypeStruct((planes * width, outer * LANES), f32)
    whole = lambda table: pl.BlockSpec(table.shape, lambda plane, step: (0, 0))
    return pl.pallas_call(
        functools.partial(finish_kernel, outer, first),
        out_shape=(shape, shape),
        grid=(planes, steps),
        in_specs=[whole(table) for table in tables]
        + [pl.BlockSpec((sources, 1, 2, rows, width), lambda plane, step: (0, plane, 0, 0, 0))]
        + [
            pl.BlockSpec((part.shape[0], 2, tile, LANES), lambda plane, step: (0, 0, plane * steps + step, 0))
            for part in parts
        ],
        out_specs=(pl.BlockSpec((tile, outer * LANES), lambda plane, step: (plane * steps + step, 0)),) * 2,
        scratch_shapes=[
            pltpu.VMEM((radix, outer // radix, 2, 8, LANES), f32),
            pltpu.VMEM((count, 2, width, LANES), f32),
        ]
        + [pltpu.VMEM((sources * rows + count, width), f32)] * 2,
        compiler_params=pltpu.CompilerParams(vmem_limit_bytes=60 * 1024 * 1024),
        name="column_finish",
    )(*tables, gathered, *parts)


def local(mantissa, exponents):
    slabs, cols = lax.axis_size("rows"), lax.axis_size("cols")
    half = cols // 2
    z = lax.axis_index("cols")
    kind, side = z % half, z // half
    local_rows, local_cols = mantissa.shape
    total = local_cols * cols
    outer = total // LANES
    slab = total // (slabs * cols)
    inner = outer // slabs
    kept = inner // 2
    lines = local_rows // outer
    kind_lines = lines // half
    chunks = kind_lines * outer // LANES
    count = outer // chunks

    index = np.arange(LANES)
    angle = 2 * np.pi * (index[:, None] * index[None, :] % LANES) / LANES
    row_matrix = np.concatenate((np.cos(angle), -np.sin(angle)), axis=1)
    column_matrix = np.block([[np.cos(angle), -np.sin(angle)], [np.sin(angle), np.cos(angle)]])
    sides = np.arange(2)[:, None, None] * kept * LANES
    twist = np.arange(outer)[None, :, None] * (index[None, None, :] + sides) % total
    twist = 2 * np.pi * twist / total
    own_side = lambda table: lax.dynamic_index_in_dim(jnp.asarray(table, f32), side, 0, False)
    row_tables = (*split_np(row_matrix / UNITS), own_side(np.cos(twist)), own_side(np.sin(twist)))
    column_tables = (
        *split_np(column_matrix),
        np.asarray(np.cos(twist[0]) / total, np.float32),
        np.asarray(np.sin(twist[0]) / total, np.float32),
    )

    scaling = jnp.exp2(exponents.astype(f32)) * UNITS
    scaling = lax.dynamic_slice_in_dim(scaling, z * (local_cols // BLOCK_COLS), local_cols // BLOCK_COLS, 1)
    scales = scaling.reshape(half, kind_lines, chunks, count // BLOCK_ROWS, -1).transpose(2, 0, 1, 3, 4)
    scales = jnp.repeat(scales.reshape(chunks, half, kind_lines * (count // BLOCK_ROWS), -1), BLOCK_COLS, axis=-1)

    by_kind = mantissa.reshape(half, kind_lines, chunks, count, local_cols)
    word = jnp.full((1,), z, jnp.int32)
    groups = [
        [row * cols + col for row in range(slabs) for col in range(part * half, (part + 1) * half)]
        for part in range(2)
    ]
    width = min(slab, LANES)
    planes = slab // width

    def exchange(spectra):
        rows = spectra.shape[3]
        if slab >= LANES:
            spectra = spectra.reshape(slabs * half, planes, 2, rows, LANES)
        else:
            spectra = spectra.reshape(slabs, kept, 2, rows, LANES // slab, slab)
            spectra = spectra.transpose(0, 1, 4, 2, 3, 5).reshape(slabs * half, 1, 2, rows, slab)
        return lax.all_to_all(
            spectra, ("rows", "cols"), split_axis=0, concat_axis=0, tiled=True, axis_index_groups=groups
        )

    order = [(chunk, 0, count) for chunk in (*range(1, chunks), 0)]
    places = len(order)
    raw, gathered, parts = {}, {}, {}

    def send(place, source):
        steps = step_rows(source, by_kind, scales, halo, *order[place])
        raw[place] = [
            lax.ppermute(steps[step % half], "cols", [(at, at ^ step) for at in range(cols)]) if step else steps[0]
            for step in range(cols)
        ]

    def mix(place):
        chunk, offset, size = order[place]
        first = chunk * count + offset
        parts[first] = mix_columns(gathered[place], column_tables, first, size)

    halo = jnp.zeros((half, 1, local_cols), f32)
    if places > 1:
        send(0, word)
    last, _ = lax.optimization_barrier((by_kind[:, -1, -1, -1], raw[0][0] if raw else word))
    ends = last.astype(f32) * scales[-1, :, -1]
    above = lax.ppermute(ends[-1:].astype(bf16), "rows", [(at, at + 1) for at in range(slabs - 1)])
    halo = jnp.concatenate((above.astype(f32), ends[:-1]), axis=0).reshape(half, 1, local_cols)

    for place in range(places > 1, min(2, places)):
        send(place, word)
    for place in range(places):
        if 0 < place < places - 1:
            source, *_ = lax.optimization_barrier((word, raw[place][3 % cols]))
            send(place + 1, source)
        spectra = transform_rows(word, raw[place], row_tables, slabs, kept, outer)
        if place >= 1:
            spectra, gathered[place - 1] = lax.optimization_barrier((spectra, gathered[place - 1]))
            mix(place - 1)
        gathered[place] = exchange(spectra)
    last = order[-1][0] * count
    parts = [parts[first] for first in sorted(parts)]
    return tuple(finish_columns(gathered[places - 1], column_tables, last, count, parts, outer))


def solution(mesh):
    in_specs = (P("rows", "cols"), P("rows", None))
    out_specs = (P(("rows", "cols"), None), P(("rows", "cols"), None))
    return jax.shard_map(local, mesh=mesh, in_specs=in_specs, out_specs=out_specs, check_vma=False)
```

```python
import functools
import math

import jax
import jax.numpy as jnp
import numpy as np
from jax import lax
from jax.experimental import pallas as pl
from jax.experimental.pallas import tpu as pltpu
from jax.sharding import PartitionSpec as P

LANES = 128
BLOCK_ROWS = 16
BLOCK_COLS = 128
UNITS = 2048
PAD = 8
f32 = jnp.float32
bf16 = jnp.bfloat16


def split(value):
    high = value.astype(bf16)
    return high, (value - high.astype(f32)).astype(bf16)


def split_np(table):
    high = np.asarray(table, np.float32).astype(jnp.bfloat16)
    return high, (np.asarray(table, np.float32) - high.astype(np.float32)).astype(jnp.bfloat16)


def product(left, right):
    return lax.dot_general(left, right, (((1,), (0,)), ((), ())), preferred_element_type=f32)


def product3(value, high, low):
    value_high, value_low = split(value)
    if value.shape[1] == LANES:
        both = jnp.concatenate((value_high, value_low), axis=1)
        return product(both, jnp.concatenate((high, high), axis=0)) + product(value_high, low)
    return product(value_high, high) + product(value_low, high) + product(value_high, low)


def times(value, angle_part, whole):
    real, imag = value
    angle_part %= whole
    if angle_part == 0:
        return real, imag
    if 4 * angle_part == whole:
        return imag, -real
    if 2 * angle_part == whole:
        return -real, -imag
    if 4 * angle_part == 3 * whole:
        return -imag, real
    if 8 * angle_part == whole:
        c = math.sqrt(0.5)
        return (real + imag) * c, (imag - real) * c
    if 8 * angle_part == 3 * whole:
        c = math.sqrt(0.5)
        return (imag - real) * c, (real + imag) * -c
    c, s = math.cos(2 * math.pi * angle_part / whole), math.sin(2 * math.pi * angle_part / whole)
    return real * c + imag * s, imag * c - real * s


def dft(values, keep=None):
    count = len(values)
    keep = count if keep is None else keep
    if count == 1:
        return values[:keep]
    half = count // 2
    even, odd = dft(values[0::2], min(keep, half)), dft(values[1::2], min(keep, half))
    odd = [times(odd[k], k, count) for k in range(len(odd))]
    low = [(e[0] + o[0], e[1] + o[1]) for e, o in zip(even, odd)]
    high = [(e[0] - o[0], e[1] - o[1]) for e, o in zip(even, odd)]
    return (low + high)[:keep]


def step_kernel(first, offset, z_ref, scale_ref, before_scale_ref, halo_ref, now_ref, before_ref, *out_refs):
    lines, _, segment, width = now_ref.shape[1:]
    groups = segment // BLOCK_ROWS
    size = out_refs[0].shape[0] // lines
    starts = lax.broadcasted_iota(jnp.int32, (segment, LANES), 0) == 0

    def take(block, carry, out_ref):
        here = pl.ds(pl.multiple_of(block * LANES, LANES), LANES)
        last = halo_ref[0, :, here]
        for line in range(lines):
            value = now_ref[0, line, 0, :, here].astype(f32).reshape(groups, BLOCK_ROWS, LANES)
            scale = scale_ref[0, line * groups : (line + 1) * groups, here]
            value = (value * scale[:, None, :]).reshape(segment, LANES)
            ends = before_ref[0, line, 0, segment - BLOCK_ROWS : segment, here].astype(f32)
            ends = ends[BLOCK_ROWS - 1 : BLOCK_ROWS] * before_scale_ref[0, (line + 1) * groups - 1 : (line + 1) * groups, here]
            above = last if first else ends
            last = ends
            change = value - jnp.where(starts, above, pltpu.roll(value, 1, 0))
            change = change[offset : offset + size].astype(jnp.int32).astype(jnp.int16)
            out_ref[line * size : (line + 1) * size, here] = change
        return carry

    for k, out_ref in enumerate(out_refs):

        @pl.when(pl.program_id(0) == k)
        def _(out_ref=out_ref):
            lax.fori_loop(0, width // LANES, functools.partial(take, out_ref=out_ref), 0)


def step_rows(z, by_kind, scales, halo, chunk, offset, size):
    kinds, lines, chunks, segment, width = by_kind.shape
    before = (chunk - 1) % chunks
    kind = lambda k, z: lax.rem(lax.bitwise_xor(z[0], k), kinds)
    block = (1, lines, 1, segment, width)
    row_block = (1,) + scales.shape[2:]
    return pl.pallas_call(
        functools.partial(step_kernel, chunk == 0, offset),
        out_shape=[jax.ShapeDtypeStruct((lines * size, width), jnp.int16)] * kinds,
        grid_spec=pltpu.PrefetchScalarGridSpec(
            num_scalar_prefetch=1,
            grid=(kinds,),
            in_specs=[
                pl.BlockSpec(row_block, lambda k, z: (kind(k, z), 0, 0)),
                pl.BlockSpec(row_block, lambda k, z: (kind(k, z), 0, 0)),
                pl.BlockSpec((1, 1, width), lambda k, z: (kind(k, z), 0, 0)),
                pl.BlockSpec(block, lambda k, z: (kind(k, z), 0, chunk, 0, 0)),
                pl.BlockSpec(block, lambda k, z: (kind(k, z), 0, before, 0, 0)),
            ],
            out_specs=[pl.BlockSpec((lines * size, width), lambda k, z: (0, 0))] * kinds,
        ),
        compiler_params=pltpu.CompilerParams(vmem_limit_bytes=20 * 1024 * 1024),
        cost_estimate=pl.CostEstimate(
            flops=0, bytes_accessed=1024, transcendentals=0
        ),
        name="step_rows",
    )(z, scales[chunk], scales[before], halo, by_kind, by_kind)


SMALLEST = -22
STEPS = 32000.0 / (15 - SMALLEST)


def encode(value):
    size = jnp.maximum(jnp.abs(value), 2.0 ** SMALLEST)
    code = (jnp.log2(size) - SMALLEST) * STEPS + 0.5
    return jnp.where(value < 0, -code, code).astype(jnp.int32).astype(jnp.int16)


def decode(code):
    code = code.astype(jnp.int32).astype(f32)
    size = jnp.abs(code)
    value = jnp.where(size > 0, jnp.exp2(size * (1 / STEPS) + SMALLEST), 0.0)
    return jnp.where(code < 0, -value, value)


def row_kernel(cols, z_ref, high_ref, low_ref, cos_ref, sin_ref, *refs):
    pieces, out_refs, (table, mixed, stage) = refs[:cols], refs[cols:-3], refs[-3:]
    rows, piece_cols = pieces[0].shape
    outer = cos_ref.shape[0]
    split_by = len(out_refs)
    slabs, kept = out_refs[0].shape[0], out_refs[0].shape[1] * split_by
    pad = PAD
    z = z_ref[0]
    table[0:pad, :] = jnp.zeros((pad, rows), f32)

    for step, piece in enumerate(pieces):
        base = lax.bitwise_xor(z, step) * piece_cols

        def turn(block, carry, piece=piece, base=base):
            here = pl.multiple_of(block * LANES, LANES)
            value = piece[:, pl.ds(here, LANES)].astype(jnp.int32).astype(f32)
            table[pl.ds(pl.multiple_of(pad + base + here, 8), LANES), :] = value.T
            return carry

        lax.fori_loop(0, piece_cols // LANES, turn, 0, unroll=8)

    def mix(index, carry):
        now = table[pl.ds(pad + index, LANES, stride=outer), :]
        before = table[pl.ds(pad + index - 1, LANES, stride=outer), :]
        spun = product3((now - before).T, high_ref[...], low_ref[...])
        real, imag = spun[:, :LANES], spun[:, LANES:]
        cos, sin = cos_ref[pl.ds(index, 1), :], sin_ref[pl.ds(index, 1), :]
        mixed[index, 0] = real * cos + imag * sin
        mixed[index, 1] = imag * cos - real * sin
        return carry

    lax.fori_loop(0, outer, mix, 0, unroll=8)

    inner = outer // slabs

    def finish(tile, carry):
        here = pl.ds(pl.multiple_of(tile * 16, 16), 16)
        for low in range(slabs):
            values = [
                (mixed[high * slabs + low, 0, here, :], mixed[high * slabs + low, 1, here, :])
                for high in range(inner)
            ]
            for k, value in enumerate(dft(values, kept)):
                stage[k, low, 0], stage[k, low, 1] = times(value, low * k, outer)
        for k in range(kept):
            out_ref, place = out_refs[k % split_by], k // split_by
            for slab, value in enumerate(dft([(stage[k, low, 0], stage[k, low, 1]) for low in range(slabs)])):
                out_ref[slab, place, 0, here, :], out_ref[slab, place, 1, here, :] = encode(value[0]), encode(value[1])
        return carry

    lax.fori_loop(0, rows // 16, finish, 0)


def transform_rows(z, pieces, tables, slabs, kept, outer, split_by=1):
    rows, piece_cols = pieces[0].shape
    cols = len(pieces)
    total = cols * piece_cols
    vmem = pl.BlockSpec(memory_space=pltpu.VMEM)
    return pl.pallas_call(
        functools.partial(row_kernel, cols),
        out_shape=[jax.ShapeDtypeStruct((slabs, kept // split_by, 2, rows, LANES), jnp.int16)] * split_by,
        in_specs=[pl.BlockSpec(memory_space=pltpu.SMEM)] + [vmem] * (4 + cols),
        out_specs=[vmem] * split_by,
        scratch_shapes=[
            pltpu.VMEM((PAD + total + outer, rows), f32),
            pltpu.VMEM((outer, 2, rows, LANES), f32),
            pltpu.VMEM((kept, slabs, 2, 16, LANES), f32),
        ],
        compiler_params=pltpu.CompilerParams(vmem_limit_bytes=24 * 1024 * 1024),
        cost_estimate=pl.CostEstimate(
            flops=300 * rows * total * LANES, bytes_accessed=rows * total * 8, transcendentals=0
        ),
        name="row_transform",
    )(z, *tables, *pieces)


def mix_chunk(first, high_ref, low_ref, cos_ref, sin_ref, in_ref, out_ref, real, imag):
    sources, _, _, rows, width = in_ref.shape
    count = out_ref.shape[0]

    def take(source, carry):
        here = pl.ds(pl.multiple_of(source * rows, rows), rows)
        real[here, :] = decode(in_ref[source, 0, 0])
        imag[here, :] = decode(in_ref[source, 0, 1])
        return carry

    def mix(index, carry):
        here = pl.ds(index, LANES, stride=count)
        value = jnp.concatenate((real[here, :].T, imag[here, :].T), axis=1)
        spun = product3(value, high_ref[...], low_ref[...])
        spun_real, spun_imag = spun[:, :LANES], spun[:, LANES:]
        cos, sin = cos_ref[pl.ds(first + index, 1), :], sin_ref[pl.ds(first + index, 1), :]
        out_ref[index, 0] = spun_real * cos + spun_imag * sin
        out_ref[index, 1] = spun_imag * cos - spun_real * sin
        return carry

    lax.fori_loop(0, sources, take, 0)
    lax.fori_loop(0, count, mix, 0, unroll=8)


def mix_columns(gathered, tables, first, count):
    sources, planes, _, rows, width = gathered.shape
    whole = lambda table: pl.BlockSpec(table.shape, lambda plane: (0, 0))
    return pl.pallas_call(
        functools.partial(mix_chunk, first),
        out_shape=jax.ShapeDtypeStruct((count, 2, planes * width, LANES), f32),
        grid=(planes,),
        in_specs=[whole(table) for table in tables]
        + [pl.BlockSpec((sources, 1, 2, rows, width), lambda plane: (0, plane, 0, 0, 0))],
        out_specs=pl.BlockSpec((count, 2, width, LANES), lambda plane: (0, 0, plane, 0)),
        scratch_shapes=[pltpu.VMEM((sources * rows + count, width), f32)] * 2,
        compiler_params=pltpu.CompilerParams(vmem_limit_bytes=20 * 1024 * 1024),
        cost_estimate=pl.CostEstimate(flops=0, bytes_accessed=1024, transcendentals=0),
        name="column_mix",
    )(*tables, gathered)


def finish_kernel(outer, first, count, filled, high_ref, low_ref, cos_ref, sin_ref, in_ref, *refs):
    parts, (real_ref, imag_ref, stage, mixed, real, imag) = refs[: -6 - filled], refs[-6:]
    size = real_ref.shape[0]
    radix = 1 << ((outer.bit_length() - 1) // 2)
    rest = outer // radix

    @pl.when(pl.program_id(0) == 0)
    def _():
        mix_chunk(first, high_ref, low_ref, cos_ref, sin_ref, in_ref, mixed, real, imag)

    places = [(part, index) for part in parts for index in range(part.shape[0])]
    places[first:first] = [(mixed, index) for index in range(count)]

    def finish(tile, carry):
        here = pl.ds(pl.multiple_of(tile * 8, 8), 8)
        there = pl.ds(pl.multiple_of(pl.program_id(0) * size + tile * 8, 8), 8)

        def load(index):
            part, own = places[index]
            lines = there if part is mixed else here
            return part[own, 0, lines, :], part[own, 1, lines, :]

        for low in range(rest):
            values = dft([load(high * rest + low) for high in range(radix)])
            for k, value in enumerate(values):
                stage[k, low, 0], stage[k, low, 1] = times(value, low * k, outer)
        for k in range(radix):
            values = dft([(stage[k, low, 0], stage[k, low, 1]) for low in range(rest)])
            for high, value in enumerate(values):
                column = (k + radix * high) * LANES
                real_ref[here, column : column + LANES], imag_ref[here, column : column + LANES] = value
        return carry

    lax.fori_loop(0, size // 8, finish, 0)


def finish_columns(gathered, tables, first, count, parts, outer, plane, planes, filled):
    sources, _, _, rows, width = gathered.shape
    tile = min(64, width)
    steps = width // tile
    radix = 1 << ((outer.bit_length() - 1) // 2)
    shape = jax.ShapeDtypeStruct((planes * width, outer * LANES), f32)
    whole = lambda table: pl.BlockSpec(table.shape, lambda step: (0,) * table.ndim)
    arguments = (*tables, gathered, *parts, *filled)
    return pl.pallas_call(
        functools.partial(finish_kernel, outer, first, count, len(filled)),
        out_shape=(shape, shape),
        grid=(steps,),
        in_specs=[whole(table) for table in (*tables, gathered)]
        + [
            pl.BlockSpec((part.shape[0], 2, tile, LANES), lambda step: (0, 0, plane * steps + step, 0))
            for part in parts
        ]
        + [pl.BlockSpec(memory_space=pl.ANY)] * len(filled),
        out_specs=(pl.BlockSpec((tile, outer * LANES), lambda step: (plane * steps + step, 0)),) * 2,
        scratch_shapes=[
            pltpu.VMEM((radix, outer // radix, 2, 8, LANES), f32),
            pltpu.VMEM((count, 2, width, LANES), f32),
        ]
        + [pltpu.VMEM((sources * rows + count, width), f32)] * 2,
        input_output_aliases={len(arguments) - len(filled) + at: at for at in range(len(filled))},
        compiler_params=pltpu.CompilerParams(vmem_limit_bytes=60 * 1024 * 1024),
        cost_estimate=pl.CostEstimate(flops=0, bytes_accessed=1024, transcendentals=0),
        name="column_finish",
    )(*arguments)


def local(mantissa, exponents):
    slabs, cols = lax.axis_size("rows"), lax.axis_size("cols")
    half = cols // 2
    z = lax.axis_index("cols")
    kind, side = z % half, z // half
    local_rows, local_cols = mantissa.shape
    total = local_cols * cols
    outer = total // LANES
    slab = total // (slabs * cols)
    inner = outer // slabs
    kept = inner // 2
    lines = local_rows // outer
    kind_lines = lines // half
    chunks = kind_lines * outer // LANES
    count = outer // chunks

    index = np.arange(LANES)
    angle = 2 * np.pi * (index[:, None] * index[None, :] % LANES) / LANES
    row_matrix = np.concatenate((np.cos(angle), -np.sin(angle)), axis=1)
    column_matrix = np.block([[np.cos(angle), -np.sin(angle)], [np.sin(angle), np.cos(angle)]])
    sides = np.arange(2)[:, None, None] * kept * LANES
    twist = np.arange(outer)[None, :, None] * (index[None, None, :] + sides) % total
    twist = 2 * np.pi * twist / total
    own_side = lambda table: lax.dynamic_index_in_dim(jnp.asarray(table, f32), side, 0, False)
    row_tables = (*split_np(row_matrix / UNITS), own_side(np.cos(twist)), own_side(np.sin(twist)))
    column_tables = (
        *split_np(column_matrix),
        np.asarray(np.cos(twist[0]) / total, np.float32),
        np.asarray(np.sin(twist[0]) / total, np.float32),
    )

    scaling = jnp.exp2(exponents.astype(f32)) * UNITS
    scaling = lax.dynamic_slice_in_dim(scaling, z * (local_cols // BLOCK_COLS), local_cols // BLOCK_COLS, 1)
    scales = scaling.reshape(half, kind_lines, chunks, count // BLOCK_ROWS, -1).transpose(2, 0, 1, 3, 4)
    scales = jnp.repeat(scales.reshape(chunks, half, kind_lines * (count // BLOCK_ROWS), -1), BLOCK_COLS, axis=-1)

    by_kind = mantissa.reshape(half, kind_lines, chunks, count, local_cols)
    word = jnp.full((1,), z, jnp.int32)
    groups = [
        [row * cols + col for row in range(slabs) for col in range(part * half, (part + 1) * half)]
        for part in range(2)
    ]
    width = min(slab, LANES)
    planes = slab // width

    def exchange(spectra):
        rows = spectra.shape[3]
        if slab >= LANES:
            spectra = spectra.reshape(slabs * half, -1, 2, rows, LANES)
        else:
            spectra = spectra.reshape(slabs, kept, 2, rows, LANES // slab, slab)
            spectra = spectra.transpose(0, 1, 4, 2, 3, 5).reshape(slabs * half, 1, 2, rows, slab)
        return lax.all_to_all(
            spectra, ("rows", "cols"), split_axis=0, concat_axis=0, tiled=True, axis_index_groups=groups
        )

    order = [(chunk, 0, count) for chunk in (*range(1, chunks), 0)]
    places = len(order)
    raw, gathered, parts = {}, {}, {}

    def send(place, source):
        steps = step_rows(source, by_kind, scales, halo, *order[place])
        raw[place] = [
            lax.ppermute(steps[step % half], "cols", [(at, at ^ step) for at in range(cols)]) if step else steps[0]
            for step in range(cols)
        ]

    def mix(place):
        chunk, offset, size = order[place]
        first = chunk * count + offset
        parts[first] = mix_columns(gathered[place], column_tables, first, size)

    halo = jnp.zeros((half, 1, local_cols), f32)
    if places > 1:
        send(0, word)
    last, _ = lax.optimization_barrier((by_kind[:, -1, -1, -1], raw[0][0] if raw else word))
    ends = last.astype(f32) * scales[-1, :, -1]
    above = lax.ppermute(ends[-1:].astype(bf16), "rows", [(at, at + 1) for at in range(slabs - 1)])
    halo = jnp.concatenate((above.astype(f32), ends[:-1]), axis=0).reshape(half, 1, local_cols)

    for place in range(places > 1, min(2, places)):
        send(place, word)
    for place in range(places):
        if 0 < place < places - 1:
            source, *_ = lax.optimization_barrier((word, raw[place][3 % cols]))
            send(place + 1, source)
        spectra = transform_rows(
            word, raw[place], row_tables, slabs, kept, outer, planes if place == places - 1 else 1
        )
        if place >= 1:
            *spectra, gathered[place - 1] = lax.optimization_barrier((*spectra, gathered[place - 1]))
            mix(place - 1)
        if place < places - 1:
            if len(parts) >= 2:
                at = next(iter(parts))
                spectra[0], parts[at] = lax.optimization_barrier((spectra[0], parts[at]))
            gathered[place] = exchange(spectra[0])
    for plane in range(1, len(spectra)):
        spectra[plane], *done = lax.optimization_barrier((spectra[plane], *parts.values()))
        parts = dict(zip(parts, done))
    gathered[places - 1] = [exchange(part) for part in spectra]
    first = order[-1][0] * count
    parts = [parts[at] for at in sorted(parts)]
    filled = ()
    for plane, last in enumerate(gathered[places - 1]):
        filled = finish_columns(last, column_tables, first, count, parts, outer, plane, planes, filled)
    return tuple(filled)


def solution(mesh):
    in_specs = (P("rows", "cols"), P("rows", None))
    out_specs = (P(("rows", "cols"), None), P(("rows", "cols"), None))
    return jax.shard_map(local, mesh=mesh, in_specs=in_specs, out_specs=out_specs, check_vma=False)
```

```python
import functools
import math

import jax
import jax.numpy as jnp
import numpy as np
from jax import lax
from jax.experimental import pallas as pl
from jax.experimental.pallas import tpu as pltpu
from jax.sharding import PartitionSpec as P

LANES = 128
BLOCK_ROWS = 16
BLOCK_COLS = 128
UNITS = 2048
PAD = 8
f32 = jnp.float32
bf16 = jnp.bfloat16


def split(value):
    high = value.astype(bf16)
    return high, (value - high.astype(f32)).astype(bf16)


def split_np(table):
    high = np.asarray(table, np.float32).astype(jnp.bfloat16)
    return high, (np.asarray(table, np.float32) - high.astype(np.float32)).astype(jnp.bfloat16)


def product(left, right):
    return lax.dot_general(left, right, (((1,), (0,)), ((), ())), preferred_element_type=f32)


def product3(value, high, low):
    value_high, value_low = split(value)
    if value.shape[1] == LANES:
        both = jnp.concatenate((value_high, value_low), axis=1)
        return product(both, jnp.concatenate((high, high), axis=0)) + product(value_high, low)
    return product(value_high, high) + product(value_low, high) + product(value_high, low)


def times(value, angle_part, whole):
    real, imag = value
    angle_part %= whole
    if angle_part == 0:
        return real, imag
    if 4 * angle_part == whole:
        return imag, -real
    if 2 * angle_part == whole:
        return -real, -imag
    if 4 * angle_part == 3 * whole:
        return -imag, real
    if 8 * angle_part == whole:
        c = math.sqrt(0.5)
        return (real + imag) * c, (imag - real) * c
    if 8 * angle_part == 3 * whole:
        c = math.sqrt(0.5)
        return (imag - real) * c, (real + imag) * -c
    c, s = math.cos(2 * math.pi * angle_part / whole), math.sin(2 * math.pi * angle_part / whole)
    return real * c + imag * s, imag * c - real * s


def dft(values, keep=None):
    count = len(values)
    keep = count if keep is None else keep
    if count == 1:
        return values[:keep]
    half = count // 2
    even, odd = dft(values[0::2], min(keep, half)), dft(values[1::2], min(keep, half))
    odd = [times(odd[k], k, count) for k in range(len(odd))]
    low = [(e[0] + o[0], e[1] + o[1]) for e, o in zip(even, odd)]
    high = [(e[0] - o[0], e[1] - o[1]) for e, o in zip(even, odd)]
    return (low + high)[:keep]


def step_kernel(first, offset, z_ref, scale_ref, before_scale_ref, halo_ref, now_ref, before_ref, *out_refs):
    lines, _, segment, width = now_ref.shape[1:]
    groups = segment // BLOCK_ROWS
    size = out_refs[0].shape[0] // lines
    starts = lax.broadcasted_iota(jnp.int32, (segment, LANES), 0) == 0

    def take(block, carry, out_ref):
        here = pl.ds(pl.multiple_of(block * LANES, LANES), LANES)
        last = halo_ref[0, :, here]
        for line in range(lines):
            value = now_ref[0, line, 0, :, here].astype(f32).reshape(groups, BLOCK_ROWS, LANES)
            scale = scale_ref[0, line * groups : (line + 1) * groups, here]
            value = (value * scale[:, None, :]).reshape(segment, LANES)
            ends = before_ref[0, line, 0, segment - BLOCK_ROWS : segment, here].astype(f32)
            ends = ends[BLOCK_ROWS - 1 : BLOCK_ROWS] * before_scale_ref[0, (line + 1) * groups - 1 : (line + 1) * groups, here]
            above = last if first else ends
            last = ends
            change = value - jnp.where(starts, above, pltpu.roll(value, 1, 0))
            change = change[offset : offset + size].astype(jnp.int32).astype(jnp.int16)
            out_ref[line * size : (line + 1) * size, here] = change
        return carry

    for k, out_ref in enumerate(out_refs):

        @pl.when(pl.program_id(0) == k)
        def _(out_ref=out_ref):
            lax.fori_loop(0, width // LANES, functools.partial(take, out_ref=out_ref), 0)


def step_rows(z, by_kind, scales, halo, chunk, offset, size):
    kinds, lines, chunks, segment, width = by_kind.shape
    before = (chunk - 1) % chunks
    kind = lambda k, z: lax.rem(lax.bitwise_xor(z[0], k), kinds)
    block = (1, lines, 1, segment, width)
    row_block = (1,) + scales.shape[2:]
    return pl.pallas_call(
        functools.partial(step_kernel, chunk == 0, offset),
        out_shape=[jax.ShapeDtypeStruct((lines * size, width), jnp.int16)] * kinds,
        grid_spec=pltpu.PrefetchScalarGridSpec(
            num_scalar_prefetch=1,
            grid=(kinds,),
            in_specs=[
                pl.BlockSpec(row_block, lambda k, z: (kind(k, z), 0, 0)),
                pl.BlockSpec(row_block, lambda k, z: (kind(k, z), 0, 0)),
                pl.BlockSpec((1, 1, width), lambda k, z: (kind(k, z), 0, 0)),
                pl.BlockSpec(block, lambda k, z: (kind(k, z), 0, chunk, 0, 0)),
                pl.BlockSpec(block, lambda k, z: (kind(k, z), 0, before, 0, 0)),
            ],
            out_specs=[pl.BlockSpec((lines * size, width), lambda k, z: (0, 0))] * kinds,
        ),
        compiler_params=pltpu.CompilerParams(vmem_limit_bytes=20 * 1024 * 1024),
        cost_estimate=pl.CostEstimate(
            flops=0, bytes_accessed=1024, transcendentals=0
        ),
        name="step_rows",
    )(z, scales[chunk], scales[before], halo, by_kind, by_kind)


SMALLEST = -22
STEPS = 32000.0 / (15 - SMALLEST)


def encode(value):
    size = jnp.maximum(jnp.abs(value), 2.0 ** SMALLEST)
    code = (jnp.log2(size) - SMALLEST) * STEPS + 0.5
    return jnp.where(value < 0, -code, code).astype(jnp.int32).astype(jnp.int16)


def decode(code):
    code = code.astype(jnp.int32).astype(f32)
    size = jnp.abs(code)
    value = jnp.where(size > 0, jnp.exp2(size * (1 / STEPS) + SMALLEST), 0.0)
    return jnp.where(code < 0, -value, value)


def row_kernel(cols, z_ref, high_ref, low_ref, cos_ref, sin_ref, *refs):
    pieces, out_refs, (table, mixed, stage) = refs[:cols], refs[cols:-3], refs[-3:]
    rows, piece_cols = pieces[0].shape
    outer = cos_ref.shape[0]
    split_by = len(out_refs)
    slabs, kept = out_refs[0].shape[0], out_refs[0].shape[1] * split_by
    pad = PAD
    z = z_ref[0]
    table[0:pad, :] = jnp.zeros((pad, rows), f32)

    for step, piece in enumerate(pieces):
        base = lax.bitwise_xor(z, step) * piece_cols

        def turn(block, carry, piece=piece, base=base):
            here = pl.multiple_of(block * LANES, LANES)
            value = piece[:, pl.ds(here, LANES)].astype(jnp.int32).astype(f32)
            table[pl.ds(pl.multiple_of(pad + base + here, 8), LANES), :] = value.T
            return carry

        lax.fori_loop(0, piece_cols // LANES, turn, 0, unroll=8)

    def mix(index, carry):
        now = table[pl.ds(pad + index, LANES, stride=outer), :]
        before = table[pl.ds(pad + index - 1, LANES, stride=outer), :]
        spun = product3((now - before).T, high_ref[...], low_ref[...])
        real, imag = spun[:, :LANES], spun[:, LANES:]
        cos, sin = cos_ref[pl.ds(index, 1), :], sin_ref[pl.ds(index, 1), :]
        mixed[index, 0] = real * cos + imag * sin
        mixed[index, 1] = imag * cos - real * sin
        return carry

    lax.fori_loop(0, outer, mix, 0, unroll=8)

    inner = outer // slabs

    def finish(tile, carry):
        here = pl.ds(pl.multiple_of(tile * 16, 16), 16)
        for low in range(slabs):
            values = [
                (mixed[high * slabs + low, 0, here, :], mixed[high * slabs + low, 1, here, :])
                for high in range(inner)
            ]
            for k, value in enumerate(dft(values, kept)):
                stage[k, low, 0], stage[k, low, 1] = times(value, low * k, outer)
        for k in range(kept):
            out_ref, place = out_refs[k % split_by], k // split_by
            for slab, value in enumerate(dft([(stage[k, low, 0], stage[k, low, 1]) for low in range(slabs)])):
                out_ref[slab, place, 0, here, :], out_ref[slab, place, 1, here, :] = encode(value[0]), encode(value[1])
        return carry

    lax.fori_loop(0, rows // 16, finish, 0)


def transform_rows(z, pieces, tables, slabs, kept, outer, split_by=1):
    rows, piece_cols = pieces[0].shape
    cols = len(pieces)
    total = cols * piece_cols
    vmem = pl.BlockSpec(memory_space=pltpu.VMEM)
    return pl.pallas_call(
        functools.partial(row_kernel, cols),
        out_shape=[jax.ShapeDtypeStruct((slabs, kept // split_by, 2, rows, LANES), jnp.int16)] * split_by,
        in_specs=[pl.BlockSpec(memory_space=pltpu.SMEM)] + [vmem] * (4 + cols),
        out_specs=[vmem] * split_by,
        scratch_shapes=[
            pltpu.VMEM((PAD + total + outer, rows), f32),
            pltpu.VMEM((outer, 2, rows, LANES), f32),
            pltpu.VMEM((kept, slabs, 2, 16, LANES), f32),
        ],
        compiler_params=pltpu.CompilerParams(vmem_limit_bytes=24 * 1024 * 1024),
        cost_estimate=pl.CostEstimate(
            flops=300 * rows * total * LANES, bytes_accessed=rows * total * 8, transcendentals=0
        ),
        name="row_transform",
    )(z, *tables, *pieces)


def mix_chunk(first, high_ref, low_ref, cos_ref, sin_ref, in_ref, out_ref, real, imag):
    sources, _, _, rows, width = in_ref.shape
    count = out_ref.shape[0]

    def take(source, carry):
        here = pl.ds(pl.multiple_of(source * rows, rows), rows)
        real[here, :] = decode(in_ref[source, 0, 0])
        imag[here, :] = decode(in_ref[source, 0, 1])
        return carry

    def mix(index, carry):
        here = pl.ds(index, LANES, stride=count)
        value = jnp.concatenate((real[here, :].T, imag[here, :].T), axis=1)
        spun = product3(value, high_ref[...], low_ref[...])
        spun_real, spun_imag = spun[:, :LANES], spun[:, LANES:]
        cos, sin = cos_ref[pl.ds(first + index, 1), :], sin_ref[pl.ds(first + index, 1), :]
        out_ref[index, 0] = spun_real * cos + spun_imag * sin
        out_ref[index, 1] = spun_imag * cos - spun_real * sin
        return carry

    lax.fori_loop(0, sources, take, 0)
    lax.fori_loop(0, count, mix, 0, unroll=8)


def mix_columns(gathered, tables, first, count):
    sources, planes, _, rows, width = gathered.shape
    whole = lambda table: pl.BlockSpec(table.shape, lambda plane: (0, 0))
    return pl.pallas_call(
        functools.partial(mix_chunk, first),
        out_shape=jax.ShapeDtypeStruct((count, 2, planes * width, LANES), f32),
        grid=(planes,),
        in_specs=[whole(table) for table in tables]
        + [pl.BlockSpec((sources, 1, 2, rows, width), lambda plane: (0, plane, 0, 0, 0))],
        out_specs=pl.BlockSpec((count, 2, width, LANES), lambda plane: (0, 0, plane, 0)),
        scratch_shapes=[pltpu.VMEM((sources * rows + count, width), f32)] * 2,
        compiler_params=pltpu.CompilerParams(vmem_limit_bytes=60 * 1024 * 1024),
        cost_estimate=pl.CostEstimate(flops=0, bytes_accessed=1024, transcendentals=0),
        name="column_mix",
    )(*tables, gathered)


def finish_kernel(outer, first, count, filled, high_ref, low_ref, cos_ref, sin_ref, in_ref, *refs):
    parts, (real_ref, imag_ref, stage, mixed, real, imag) = refs[: -6 - filled], refs[-6:]
    size = real_ref.shape[0]
    radix = 1 << ((outer.bit_length() - 1) // 2)
    rest = outer // radix

    @pl.when(pl.program_id(0) == 0)
    def _():
        mix_chunk(first, high_ref, low_ref, cos_ref, sin_ref, in_ref, mixed, real, imag)

    places = [(part, index) for part in parts for index in range(part.shape[0])]
    places[first:first] = [(mixed, index) for index in range(count)]

    def finish(tile, carry):
        here = pl.ds(pl.multiple_of(tile * 8, 8), 8)
        there = pl.ds(pl.multiple_of(pl.program_id(0) * size + tile * 8, 8), 8)

        def load(index):
            part, own = places[index]
            lines = there if part is mixed else here
            return part[own, 0, lines, :], part[own, 1, lines, :]

        for low in range(rest):
            values = dft([load(high * rest + low) for high in range(radix)])
            for k, value in enumerate(values):
                stage[k, low, 0], stage[k, low, 1] = times(value, low * k, outer)
        for k in range(radix):
            values = dft([(stage[k, low, 0], stage[k, low, 1]) for low in range(rest)])
            for high, value in enumerate(values):
                column = (k + radix * high) * LANES
                real_ref[here, column : column + LANES], imag_ref[here, column : column + LANES] = value
        return carry

    lax.fori_loop(0, size // 8, finish, 0)


def finish_columns(gathered, tables, first, count, parts, outer, plane, planes, filled):
    sources, _, _, rows, width = gathered.shape
    tile = min(64, width)
    steps = width // tile
    radix = 1 << ((outer.bit_length() - 1) // 2)
    shape = jax.ShapeDtypeStruct((planes * width, outer * LANES), f32)
    whole = lambda table: pl.BlockSpec(table.shape, lambda step: (0,) * table.ndim)
    arguments = (*tables, gathered, *parts, *filled)
    return pl.pallas_call(
        functools.partial(finish_kernel, outer, first, count, len(filled)),
        out_shape=(shape, shape),
        grid=(steps,),
        in_specs=[whole(table) for table in (*tables, gathered)]
        + [
            pl.BlockSpec((part.shape[0], 2, tile, LANES), lambda step: (0, 0, plane * steps + step, 0))
            for part in parts
        ]
        + [pl.BlockSpec(memory_space=pl.ANY)] * len(filled),
        out_specs=(pl.BlockSpec((tile, outer * LANES), lambda step: (plane * steps + step, 0)),) * 2,
        scratch_shapes=[
            pltpu.VMEM((radix, outer // radix, 2, 8, LANES), f32),
            pltpu.VMEM((count, 2, width, LANES), f32),
        ]
        + [pltpu.VMEM((sources * rows + count, width), f32)] * 2,
        input_output_aliases={len(arguments) - len(filled) + at: at for at in range(len(filled))},
        compiler_params=pltpu.CompilerParams(vmem_limit_bytes=60 * 1024 * 1024),
        cost_estimate=pl.CostEstimate(flops=0, bytes_accessed=1024, transcendentals=0),
        name="column_finish",
    )(*arguments)


def local(mantissa, exponents):
    slabs, cols = lax.axis_size("rows"), lax.axis_size("cols")
    half = cols // 2
    z = lax.axis_index("cols")
    kind, side = z % half, z // half
    local_rows, local_cols = mantissa.shape
    total = local_cols * cols
    outer = total // LANES
    slab = total // (slabs * cols)
    inner = outer // slabs
    kept = inner // 2
    lines = local_rows // outer
    kind_lines = lines // half
    chunks = kind_lines * outer // LANES
    count = outer // chunks

    index = np.arange(LANES)
    angle = 2 * np.pi * (index[:, None] * index[None, :] % LANES) / LANES
    row_matrix = np.concatenate((np.cos(angle), -np.sin(angle)), axis=1)
    column_matrix = np.block([[np.cos(angle), -np.sin(angle)], [np.sin(angle), np.cos(angle)]])
    sides = np.arange(2)[:, None, None] * kept * LANES
    twist = np.arange(outer)[None, :, None] * (index[None, None, :] + sides) % total
    twist = 2 * np.pi * twist / total
    own_side = lambda table: lax.dynamic_index_in_dim(jnp.asarray(table, f32), side, 0, False)
    row_tables = (*split_np(row_matrix / UNITS), own_side(np.cos(twist)), own_side(np.sin(twist)))
    column_tables = (
        *split_np(column_matrix),
        np.asarray(np.cos(twist[0]) / total, np.float32),
        np.asarray(np.sin(twist[0]) / total, np.float32),
    )

    scaling = jnp.exp2(exponents.astype(f32)) * UNITS
    scaling = lax.dynamic_slice_in_dim(scaling, z * (local_cols // BLOCK_COLS), local_cols // BLOCK_COLS, 1)
    scales = scaling.reshape(half, kind_lines, chunks, count // BLOCK_ROWS, -1).transpose(2, 0, 1, 3, 4)
    scales = jnp.repeat(scales.reshape(chunks, half, kind_lines * (count // BLOCK_ROWS), -1), BLOCK_COLS, axis=-1)

    by_kind = mantissa.reshape(half, kind_lines, chunks, count, local_cols)
    word = jnp.full((1,), z, jnp.int32)
    groups = [
        [row * cols + col for row in range(slabs) for col in range(part * half, (part + 1) * half)]
        for part in range(2)
    ]
    width = min(slab, LANES)
    planes = slab // width

    def exchange(spectra):
        rows = spectra.shape[3]
        if slab >= LANES:
            spectra = spectra.reshape(slabs * half, -1, 2, rows, LANES)
        else:
            spectra = spectra.reshape(slabs, kept, 2, rows, LANES // slab, slab)
            spectra = spectra.transpose(0, 1, 4, 2, 3, 5).reshape(slabs * half, 1, 2, rows, slab)
        return lax.all_to_all(
            spectra, ("rows", "cols"), split_axis=0, concat_axis=0, tiled=True, axis_index_groups=groups
        )

    order = [(chunk, 0, count) for chunk in (*range(1, chunks), 0)]
    places = len(order)
    raw, gathered, parts = {}, {}, {}

    def send(place, source):
        steps = step_rows(source, by_kind, scales, halo, *order[place])
        raw[place] = [
            lax.ppermute(steps[step % half], "cols", [(at, at ^ step) for at in range(cols)]) if step else steps[0]
            for step in range(cols)
        ]

    def mix(place):
        chunk, offset, size = order[place]
        first = chunk * count + offset
        parts[first] = mix_columns(gathered[place], column_tables, first, size)

    halo = jnp.zeros((half, 1, local_cols), f32)
    if places > 1:
        send(0, word)
    last, _ = lax.optimization_barrier((by_kind[:, -1, -1, -1], raw[0][0] if raw else word))
    ends = last.astype(f32) * scales[-1, :, -1]
    above = lax.ppermute(ends[-1:].astype(bf16), "rows", [(at, at + 1) for at in range(slabs - 1)])
    halo = jnp.concatenate((above.astype(f32), ends[:-1]), axis=0).reshape(half, 1, local_cols)

    for place in range(places > 1, min(2, places)):
        send(place, word)
    for place in range(places):
        if 0 < place < places - 1:
            source, *_ = lax.optimization_barrier((word, raw[place][3 % cols]))
            send(place + 1, source)
        spectra = transform_rows(
            word, raw[place], row_tables, slabs, kept, outer, planes if place == places - 1 else 1
        )
        if place >= 1:
            *spectra, gathered[place - 1] = lax.optimization_barrier((*spectra, gathered[place - 1]))
            mix(place - 1)
        if place < places - 1:
            if len(parts) >= 2:
                at = next(iter(parts))
                spectra[0], parts[at] = lax.optimization_barrier((spectra[0], parts[at]))
            gathered[place] = exchange(spectra[0])
    for plane in range(1, len(spectra)):
        spectra[plane], *done = lax.optimization_barrier((spectra[plane], *parts.values()))
        parts = dict(zip(parts, done))
    gathered[places - 1] = [exchange(part) for part in spectra]
    first = order[-1][0] * count
    parts = [parts[at] for at in sorted(parts)]
    filled = ()
    for plane, last in enumerate(gathered[places - 1]):
        filled = finish_columns(last, column_tables, first, count, parts, outer, plane, planes, filled)
    return tuple(filled)


def solution(mesh):
    in_specs = (P("rows", "cols"), P("rows", None))
    out_specs = (P(("rows", "cols"), None), P(("rows", "cols"), None))
    return jax.shard_map(local, mesh=mesh, in_specs=in_specs, out_specs=out_specs, check_vma=False)
```
